128 devices in a mesh: line: 8 (over y, core), block: 16 (over z, x).
Axes of the slice: x: 4, y: 4, z: 4, core: 2. Of those that a mesh axis runs over, the one named last changes fastest.
Arguments:
- residual: float32 [6, 64, 15, 2048], P(None, 'line', None, 'block'), may hold values from -6 to 6
- adjoint: float32 [6, 64, 15, 2048], P(None, 'line', None, 'block'), may hold values from -6 to 6
- i_factors: float32 [16, 2, 6, 64, 8], P('block', None, None, 'line'), as said below
- k_factors: float32 [8, 2, 6, 2048, 128], P('line', None, None, 'block'), as said below
- couplings: float32 [8, 16, 4, 3, 6], P('line', 'block')
- receptor_cell: int32 [8, 16, 16, 2048], P('line', 'block'), may hold values from 0 to 15359
- send_count: int32 [8, 16, 16], P('line', 'block'), may hold values from 512 to 2048, as said below
- donor_cell: int32 [8, 16, 16, 2048], P('line', 'block'), may hold values from 0 to 13310, as said below
- donor_weight: float32 [8, 16, 3, 16, 2048], P('line', 'block'), may hold values from 0 to 1
Outputs:
- update: float32 [6, 64, 15, 2048], P(None, 'line', None, 'block')
The draws below stay inside these ranges and needn't reach their ends.
Inputs may be any that keep to these rules, and one draw needn't show every extreme that they name: The first send_count slots of each device for each donor owner are live. In each group along block one donor owner receives exactly 2048 live slots from every source device of the group; every other owner receives at most 1280 live slots from each source, and some source sends exactly that many to some owner. `donor_cell`: numbered within the owner's block; its base cell has i < 7, j < 14 and k < 127 in the block, so that all eight donor cells lie in the block. `receptor_cell`: numbered within the sending device's block; entries of slots that are not live are arbitrary. `i_factors`: each segment matrix is lower triangular with a diagonal between 0.8 and 1.2. `k_factors`: each segment matrix is lower triangular with a diagonal between 0.8 and 1.2.
All inputs are finite; a program needn't handle non-finite values.
Results may differ from the reference program's by a relative error of at most 0.00022.
Values sent between devices are 32-bit elements; how exact they have to be, the bound alone decides.
A program may use at most 320 MiB of HBM per device.

```python
import jax
import jax.numpy as jnp
from jax import lax

FIELD_COUNT = 6
CI = 8
CJ = 15
CK = 128
CAP = 2048
NI = 64
NJ = 15
NK = 2048
N_LINE = 8
N_BLOCK = 16


def make_factor(key, leading, segments, length, chain_count):
    lookup_keys = jax.random.split(key, 6)
    slow_count = 3
    ranks = jnp.stack([jax.random.permutation(lookup_keys[0], FIELD_COUNT), jax.random.permutation(lookup_keys[1], FIELD_COUNT)])
    slow_field = (ranks < slow_count)[None, :, :, None, None, None]
    rate_shape = (leading, 2, FIELD_COUNT, segments, 1, 1)
    slow_rate = jnp.exp(jax.random.uniform(lookup_keys[2], rate_shape, jnp.float32, jnp.log(0.3), jnp.log(1.2))) / (length * chain_count)
    fast_rate = jnp.exp(jax.random.uniform(lookup_keys[3], rate_shape, jnp.float32, jnp.log(1.5), jnp.log(2.5))) / min(length, 40)
    rate = jnp.where(slow_field, slow_rate, fast_rate)
    row_index = jnp.arange(length)[:, None]
    col_index = jnp.arange(length)[None, :]
    distance = jnp.maximum(row_index - col_index, 0).astype(jnp.float32)
    full_shape = (leading, 2, FIELD_COUNT, segments, length, length)
    jitter = jax.random.uniform(lookup_keys[4], full_shape, jnp.float32, 0.85, 1.15)
    below = jnp.exp(-rate * distance) * jitter / jnp.sqrt(jnp.float32(length))
    diagonal = jax.random.uniform(lookup_keys[5], full_shape, jnp.float32, 0.8, 1.2)
    matrix = jnp.where(row_index > col_index, below, jnp.where(row_index == col_index, diagonal, 0.0))
    return matrix.reshape(leading, 2, FIELD_COUNT, segments * length, length)


def draw_i_factors(key, part):
    return make_factor(key, N_BLOCK, N_LINE, CI, N_LINE)


def draw_k_factors(key, part):
    return make_factor(key, N_LINE, N_BLOCK, CK, N_BLOCK)


def draw_couplings(key, part):
    lookup_keys = jax.random.split(key, 3)
    lowest = jnp.array([0.4, 0.05, 0.3], jnp.float32).reshape(1, 1, 1, 3, 1)
    highest = jnp.array([0.55, 0.12, 0.45], jnp.float32).reshape(1, 1, 1, 3, 1)
    shape = (N_LINE, N_BLOCK, 4, 3, FIELD_COUNT)
    spread = jax.random.uniform(lookup_keys[0], shape, jnp.float32)
    table_entries = lowest + (highest - lowest) * spread
    chain_lengths = jnp.array([CI, CI, CK, CK], jnp.float32).reshape(1, 1, 4, 1, 1)
    group_selection = jax.random.uniform(lookup_keys[1], (N_LINE, N_BLOCK, 4, 1, FIELD_COUNT), jnp.float32)
    group_length = jax.random.uniform(lookup_keys[2], (N_LINE, N_BLOCK, 4, 1, FIELD_COUNT), jnp.float32, 0.5, 0.8)
    donor_group = jnp.where(group_selection < 0.15, group_length, 1.0)
    return table_entries * jnp.sqrt(chain_lengths) * donor_group


def draw_send_count(key, part):
    lookup_keys = jax.random.split(key, 2)
    head_most = 5 * CAP // 8
    background = jax.random.randint(lookup_keys[0], (N_LINE, N_BLOCK, N_BLOCK), CAP // 4, head_most + 1)
    hottest = jax.random.randint(lookup_keys[1], (N_LINE, 1, 1), 0, N_BLOCK)
    owners = jnp.arange(N_BLOCK, dtype=jnp.int32)[None, None, :]
    second = (hottest + 1) % N_BLOCK
    background = jnp.where(owners == second, head_most, background)
    return jnp.where(owners == hottest, CAP, background).astype(jnp.int32)


def draw_donor_cell(key, part):
    lookup_keys = jax.random.split(key, 3)
    shape = (N_LINE, N_BLOCK, N_BLOCK, CAP)
    along_i = jax.random.randint(lookup_keys[0], shape, 0, CI - 1)
    along_j = jax.random.randint(lookup_keys[1], shape, 0, NJ - 1)
    along_k = jax.random.randint(lookup_keys[2], shape, 0, CK - 1)
    return (along_i * NJ * CK + along_j * CK + along_k).astype(jnp.int32)


def place_ends(drawn, stream_key, low, high):
    longest = drawn.shape.index(max(drawn.shape))
    spots = []
    for shift in (0, 1):
        where = [jax.random.randint(jax.random.fold_in(stream_key, axis), (), 0, length) for axis, length in enumerate(drawn.shape)]
        where[longest] = (where[longest] + shift) % drawn.shape[longest]
        spots.append(tuple(where))
    return drawn.at[spots[0]].set(low).at[spots[1]].set(high)


def block_levels(stream_key, shape, cuts, low, largest):
    gain, own = 1.0, jax.random.fold_in(stream_key, 6)
    for position, blocks in cuts:
        draws = jnp.exp(jax.random.uniform(jax.random.fold_in(own, position), (blocks,), jnp.float32, low / len(cuts), largest / len(cuts)))
        gain = gain * jnp.repeat(draws, shape[position] // blocks).reshape([-1 if axis == position else 1 for axis in range(len(shape))])
    return gain


def gaussian(stream_key, dims, width, most, cuts=(), held_as=jnp.bfloat16):
    drawn = jax.random.normal(stream_key, dims, jnp.float32) * width
    if len(cuts) > 0:
        drawn = block_levels(stream_key, dims, cuts, -0.22, 0.18) * drawn
    return jnp.clip(drawn, min=-most, max=most).astype(held_as)


def setup_inputs(seed: int = 0) -> dict:
    arg_keys = jax.random.split(jax.random.key(seed), 10)
    residual = gaussian(arg_keys[0], (FIELD_COUNT, NI, NJ, NK), 1.0, 6.0, ((1, 8), (3, 16)), jnp.float32)
    adjoint = gaussian(arg_keys[1], (FIELD_COUNT, NI, NJ, NK), 1.0, 6.0, ((1, 8), (3, 16)), jnp.float32)
    i_factors = draw_i_factors(jax.random.fold_in(arg_keys[9], 71), 0)
    k_factors = draw_k_factors(jax.random.fold_in(arg_keys[9], 71), 0)
    couplings = draw_couplings(jax.random.fold_in(arg_keys[9], 71), 0)
    receptor_cell = place_ends(jax.random.randint(arg_keys[5], (N_LINE, N_BLOCK, N_BLOCK, CAP), 0, CI * CJ * CK), jax.random.fold_in(arg_keys[5], 1), 0, (CI * CJ * CK) - 1).astype(jnp.int32)
    send_count = draw_send_count(jax.random.fold_in(arg_keys[9], 71), 0)
    donor_cell = draw_donor_cell(jax.random.fold_in(arg_keys[9], 71), 0)
    donor_weight = jnp.clip(1.0 * jax.random.uniform(arg_keys[8], (N_LINE, N_BLOCK, 3, N_BLOCK, CAP), jnp.float32) ** block_levels(arg_keys[8], (N_LINE, N_BLOCK, 3, N_BLOCK, CAP), ((0, 8), (1, 16)), -0.2, 0.2), 0.0, 1.0)
    return dict(residual=residual, adjoint=adjoint, i_factors=i_factors, k_factors=k_factors, couplings=couplings, receptor_cell=receptor_cell, send_count=send_count, donor_cell=donor_cell, donor_weight=donor_weight)


def coupling_matrix(triple):
    zeros_part = jnp.zeros_like(triple[..., 0, :])
    upper_row = jnp.stack([triple[..., 0, :], triple[..., 1, :]], axis=-1)
    lower_row = jnp.stack([triple[..., 2, :], zeros_part], axis=-1)
    return jnp.stack([upper_row, lower_row], axis=-2)


def chain_solve(columns, factors, couplings):
    fields = columns.shape[0]
    segments = factors.shape[0]
    length = factors.shape[2]
    incoming = jnp.zeros((fields, 2, columns.shape[2]), jnp.float32)
    pieces = []
    for segment in range(segments):
        block_data = columns[:, segment * length:(segment + 1) * length]
        homogeneous = jnp.einsum('fpq,fql->fpl', factors[segment], block_data, precision=lax.Precision.HIGHEST)
        influence = jnp.einsum('fpa,fab->fpb', factors[segment][:, :, 0:2], couplings[segment], precision=lax.Precision.HIGHEST)
        solved = homogeneous - jnp.einsum('fpa,fal->fpl', influence, incoming, precision=lax.Precision.HIGHEST)
        incoming = jnp.stack([solved[:, -1], solved[:, -2]], axis=1)
        pieces.append(solved)
    return jnp.concatenate(pieces, axis=1)


def both_ways(columns, lower, upper, couple_lower, couple_upper):
    forward = chain_solve(columns, lower, couple_lower)
    return jnp.flip(chain_solve(jnp.flip(forward, 1), upper[::-1], couple_upper[::-1]), 1)


def spread_donors(right_side, incoming, donor_cell, donor_weight, cells_j, cells_k):
    fields = right_side.shape[0]
    base_cell = donor_cell.reshape(-1)
    fractions = donor_weight.reshape(3, -1)
    values = incoming.reshape(fields, -1)
    index_list = []
    weight_list = []
    for corner in range(8):
        step_i = corner // 4
        step_j = (corner // 2) % 2
        step_k = corner % 2
        along_i = fractions[0] if step_i else 1.0 - fractions[0]
        along_j = fractions[1] if step_j else 1.0 - fractions[1]
        along_k = fractions[2] if step_k else 1.0 - fractions[2]
        weight_list.append(along_i * along_j * along_k)
        index_list.append(base_cell + step_i * cells_j * cells_k + step_j * cells_k + step_k)
    targets = jnp.concatenate(index_list)
    weights = jnp.concatenate(weight_list)
    spread = jnp.tile(values, (1, 8)) * weights[None, :]
    return right_side.at[:, targets].add(spread)


def to_blocks(grid):
    shaped = grid.reshape(FIELD_COUNT, N_LINE, CI, NJ, N_BLOCK, CK).transpose(1, 4, 0, 2, 3, 5)
    return shaped.reshape(N_LINE * N_BLOCK, FIELD_COUNT, CI * NJ * CK)


def from_blocks(blocks):
    shaped = blocks.reshape(N_LINE, N_BLOCK, FIELD_COUNT, CI, NJ, CK).transpose(2, 0, 3, 4, 1, 5)
    return shaped.reshape(FIELD_COUNT, NI, NJ, NK)


def reference(residual, adjoint, i_factors, k_factors, couplings, receptor_cell, send_count, donor_cell, donor_weight):
    adjoint_blocks = to_blocks(adjoint)
    receptors = receptor_cell.reshape(N_LINE * N_BLOCK, N_BLOCK * CAP)
    picked = lax.map(lambda pair: pair[0][:, pair[1]], (adjoint_blocks, receptors))
    picked = picked.reshape(N_LINE, N_BLOCK, FIELD_COUNT, N_BLOCK, CAP)
    active = jnp.arange(CAP, dtype=jnp.int32)[None, None, None, :] < send_count[:, :, :, None]
    outgoing = jnp.where(active[:, :, None], picked, 0.0)
    incoming = outgoing.transpose(0, 3, 2, 1, 4).reshape(N_LINE * N_BLOCK, FIELD_COUNT, N_BLOCK, CAP)
    residual_blocks = to_blocks(residual)
    combined = lax.map(
        lambda group: spread_donors(group[0], group[1], group[2], group[3], NJ, CK),
        (residual_blocks, incoming, donor_cell.reshape(N_LINE * N_BLOCK, N_BLOCK, CAP),
         donor_weight.reshape(N_LINE * N_BLOCK, 3, N_BLOCK, CAP)))
    right_side = from_blocks(combined)

    i_parts = []
    for block_index in range(N_BLOCK):
        columns = right_side[:, :, :, block_index * CK:(block_index + 1) * CK].reshape(FIELD_COUNT, NI, NJ * CK)
        lower = i_factors[block_index, 0].reshape(FIELD_COUNT, N_LINE, CI, CI).transpose(1, 0, 2, 3)
        upper = i_factors[block_index, 1].reshape(FIELD_COUNT, N_LINE, CI, CI).transpose(1, 0, 2, 3)
        couple_lower = coupling_matrix(couplings[:, block_index, 0])
        couple_upper = coupling_matrix(couplings[:, block_index, 1])
        solved = both_ways(columns, lower, upper, couple_lower, couple_upper)
        i_parts.append(solved.reshape(FIELD_COUNT, NI, NJ, CK))
    after_i = jnp.concatenate(i_parts, axis=3)

    k_parts = []
    for line_index in range(N_LINE):
        columns = after_i[:, line_index * CI:(line_index + 1) * CI].reshape(FIELD_COUNT, CI * NJ, NK).transpose(0, 2, 1)
        lower = k_factors[line_index, 0].reshape(FIELD_COUNT, N_BLOCK, CK, CK).transpose(1, 0, 2, 3)
        upper = k_factors[line_index, 1].reshape(FIELD_COUNT, N_BLOCK, CK, CK).transpose(1, 0, 2, 3)
        couple_lower = coupling_matrix(couplings[line_index, :, 2])
        couple_upper = coupling_matrix(couplings[line_index, :, 3])
        solved = both_ways(columns, lower, upper, couple_lower, couple_upper)
        k_parts.append(solved.transpose(0, 2, 1).reshape(FIELD_COUNT, CI, NJ, NK))
    return jnp.concatenate(k_parts, axis=1)
```

```python
import functools

import jax
import jax.numpy as jnp
from jax import lax
from jax.experimental import pallas as pl
from jax.experimental.pallas import tpu as pltpu
from jax.sharding import PartitionSpec as P

F32, BF = jnp.float32, jnp.bfloat16
FIELDS, CI, CJ, CK, CAP = 6, 8, 15, 128, 2048
LINES, BLOCKS = 8, 16
HIGHEST = lax.Precision.HIGHEST
MESH = pl.DeviceIdType.MESH


def iota(shape, axis):
    return lax.broadcasted_iota(jnp.int32, shape, axis)


def split(x):
    high = x.astype(BF)
    return high, (x - high.astype(F32)).astype(BF)


def as_bf(x):
    return x.astype(F32).astype(BF)


def mm(a, b):
    return jnp.dot(a, b, precision=HIGHEST, preferred_element_type=F32)


def mm_nt(a, b):
    return lax.dot_general(
        a, b, (((1,), (1,)), ((), ())), precision=HIGHEST, preferred_element_type=F32
    )


def mm_tn(a, b):
    return lax.dot_general(
        a, b, (((0,), (0,)), ((), ())), precision=HIGHEST, preferred_element_type=F32
    )


def cell_parts(cell):
    ij = cell >> 7
    i = (ij * 137) >> 11
    return i, ij - i * CJ, cell & 127


def gather_kernel(adj_ref, cell_ref, count_ref, out_ref, table, where_ref):
    for f in range(FIELDS):
        planes = [adj_ref[f, j] for j in range(CJ)] + [jnp.zeros((CI, CK), F32)]
        for half in range(2):
            high, low = split(jnp.concatenate(planes[8 * half : 8 * half + 8], 0))
            row, col = f * 64, half * CK
            table[row : row + 64, col : col + CK] = high
            table[row : row + 64, 256 + col : 256 + col + CK] = low
    i, j, k = cell_parts(cell_ref[...])
    where_ref[0] = (j & 7) * CI + i
    where_ref[1] = (j >> 3) * CK + k

    def owner(s, carry):
        C = CAP
        group = jnp.broadcast_to(where_ref[0, pl.ds(s, 1), :], (64, C))
        slot = as_bf(jnp.broadcast_to(where_ref[1, pl.ds(s, 1), :], (16, C)))
        one, zero = jnp.ones((16, C), BF), jnp.zeros((16, C), BF)
        base = iota((16, C), 0)
        hot = [jnp.where(as_bf(base + 16 * n) == slot, one, zero) for n in range(16)]
        hot = jnp.concatenate(hot, 0)
        found = jnp.dot(
            table[...], jnp.concatenate([hot, hot], 0), preferred_element_type=F32
        ).reshape(FIELDS, 64, C)
        mine = iota((64, C), 0) == group
        live = iota((1, C), 1) < count_ref[s]
        for f in range(FIELDS):
            picked = jnp.sum(jnp.where(mine, found[f], 0.0), axis=0, keepdims=True)
            out_ref[s, f : f + 1, :] = jnp.where(live, picked, 0.0)
        return carry

    lax.fori_loop(0, BLOCKS, owner, 0)


def gather(adjoint, receptor_cell, send_count):
    vmem = pl.BlockSpec(memory_space=pltpu.VMEM)
    return pl.pallas_call(
        gather_kernel,
        out_shape=jax.ShapeDtypeStruct((BLOCKS, FIELDS, CAP), F32),
        in_specs=[vmem, vmem, pl.BlockSpec(memory_space=pltpu.SMEM)],
        out_specs=vmem,
        scratch_shapes=[
            pltpu.VMEM((FIELDS * 64, 512), BF),
            pltpu.VMEM((2, BLOCKS, CAP), jnp.int32),
        ],
        compiler_params=pltpu.CompilerParams(vmem_limit_bytes=56 * 2**20),
        name="gather",
    )(adjoint, receptor_cell, send_count)


def scatter_all(inc_ref, cell_ref, weight_ref, acc, place):
    i, j, k = cell_parts(cell_ref[...])
    upper = jnp.where(j >= 7, 1, 0)
    place[0] = i
    place[1] = j - 7 * upper
    place[2] = upper * CK + k
    acc[...] = jnp.zeros_like(acc)

    def source(s, carry):
        C = CAP

        def row(ref, a, n):
            return jnp.broadcast_to(ref[a, pl.ds(s, 1), :], (n, C))

        at = iota((8, C), 0)

        def hat(base, t):
            return jnp.where(at == base, 1.0 - t, jnp.where(at == base + 1, t, 0.0))

        wi = hat(row(place, 0, 8), row(weight_ref, 0, 8))
        wj = hat(row(place, 1, 8), row(weight_ref, 1, 8))
        values = inc_ref[s]
        u = jnp.concatenate(
            [jnp.broadcast_to(values[f : f + 1], (8, C)) * wi for f in range(FIELDS)], 0
        )
        high, low = [], []
        for r in range(8):
            h, l = split(u * jnp.broadcast_to(wj[r : r + 1], (48, C)))
            high.append(h)
            low.append(l)
        high, low = jnp.concatenate(high, 0), jnp.concatenate(low, 0)
        z = row(weight_ref, 2, 16)
        z1h, z1l = split(z)
        z0h, z0l = split(1.0 - z)
        t = row(place, 2, 16)
        t0, t1 = as_bf(t), as_bf(t + 1)
        zero = jnp.zeros((16, C), BF)
        base = iota((16, C), 0)
        col_h, col_l = [], []
        for n in range(16):
            r = as_bf(base + 16 * n)
            first, second = r == t0, r == t1
            col_h.append(jnp.where(first, z0h, jnp.where(second, z1h, zero)))
            col_l.append(jnp.where(first, z0l, jnp.where(second, z1l, zero)))
        col_h, col_l = jnp.concatenate(col_h, 0), jnp.concatenate(col_l, 0)
        acc[...] += lax.dot_general(
            jnp.concatenate([high, high, low], 1),
            jnp.concatenate([col_h, col_l, col_h], 1),
            (((1,), (1,)), ((), ())),
            preferred_element_type=F32,
        )
        return carry

    lax.fori_loop(0, BLOCKS, source, 0)


def entries(shape, items):
    rows, cols = iota(shape, 0), iota(shape, 1)
    out = jnp.zeros(shape, F32)
    for r, c, value in items:
        out = jnp.where((rows == r) & (cols == c), value, out)
    return out


def prepare_i(ifac_ref, coup_ref, i_mat, i_state, i_ends, i_maps_own):
    n = FIELDS * CI
    r, c = iota((n, n), 0), iota((n, n), 1)
    same = (r >> 3) == (c >> 3)
    flip = jnp.where(same & ((r & 7) + (c & 7) == 7), 1.0, 0.0)
    spread = jnp.where(iota((CI, n), 0) == (iota((CI, n), 1) & 7), 1.0, 0.0)

    def diagonal(direction):
        flat = ifac_ref[direction].reshape(n, CI)
        return jnp.where(same, mm(flat, spread), 0.0)

    low = diagonal(0)
    up = mm(flip, mm(diagonal(1), flip))
    whole = mm(up, low)
    shape = (n, 24)
    e_low = entries(
        shape,
        [(8 * f, f, coup_ref[0, 0, f]) for f in range(FIELDS)]
        + [(8 * f, 6 + f, coup_ref[1, 0, f]) for f in range(FIELDS)]
        + [(8 * f + 1, f, coup_ref[2, 0, f]) for f in range(FIELDS)],
    )
    e_up = entries(
        shape,
        [(8 * f + 7, 12 + f, coup_ref[0, 1, f]) for f in range(FIELDS)]
        + [(8 * f + 7, 18 + f, coup_ref[1, 1, f]) for f in range(FIELDS)]
        + [(8 * f + 6, 12 + f, coup_ref[2, 1, f]) for f in range(FIELDS)],
    )
    infl_low = mm(low, e_low)
    state = -mm(up, infl_low + e_up)
    sel_shape = (24, n)
    comp = [(a, f) for a in range(2) for f in range(FIELDS)]
    sel_e = entries(sel_shape, [(a * 6 + f, 8 * f + 7 - a, 1.0) for a, f in comp])
    sel_p = entries(sel_shape, [(12 + a * 6 + f, 8 * f + a, 1.0) for a, f in comp])
    i_mat[...] = whole
    i_state[...] = state
    i_ends[...] = mm(sel_e, low) + mm(sel_p, whole)
    between = mm(sel_p, state) - mm(sel_e, infl_low)
    fold_r, fold_c = iota((24, CK), 0), iota((24, CK), 1)
    fold = jnp.where((fold_r >= 6 * fold_c) & (fold_r < 6 * fold_c + 6), 1.0, 0.0)
    i_maps_own[...] = mm(between, fold)


def prepare_k(kfac_ref, coup_ref, k_mat, k_state, k_ends, k_pad):
    n = CK
    flip = jnp.where(iota((n, n), 0) + iota((n, n), 1) == n - 1, 1.0, 0.0)
    sel_e = entries((8, n), [(0, n - 1, 1.0), (1, n - 2, 1.0)])
    sel_p = entries((8, n), [(2, 0, 1.0), (3, 1, 1.0)])

    def field(f, carry):
        low = kfac_ref[0, f]
        up = mm(flip, mm(kfac_ref[1, f], flip))
        whole = mm(up, low)
        e_low = entries(
            (8, n),
            [(0, 0, coup_ref[0, 2, f]), (0, 1, coup_ref[2, 2, f]), (1, 0, coup_ref[1, 2, f])],
        )
        e_up = entries(
            (8, n),
            [
                (2, n - 1, coup_ref[0, 3, f]),
                (2, n - 2, coup_ref[2, 3, f]),
                (3, n - 1, coup_ref[1, 3, f]),
            ],
        )
        infl_low = mm_nt(e_low, low)
        state = -mm_nt(infl_low + e_up, up)
        k_mat[f] = whole
        k_state[f] = state
        k_ends[f] = mm(sel_e, low) + mm(sel_p, whole)
        pad = jnp.zeros((n - 8, n), F32)
        k_pad[f] = mm_nt(sel_p, jnp.concatenate([pad, state], 0)) - mm_nt(
            sel_e, jnp.concatenate([pad, infl_low], 0)
        )
        return carry

    lax.fori_loop(0, FIELDS, field, 0)


def chain(count, ends, maps, keep):
    shape = ends(0)[0].shape
    s = [jnp.zeros(shape, F32)] * 2
    tops = []
    for n in range(count):
        e0, e1, p0, p1 = ends(n)
        m = maps(n)
        keep(n, 0, s)
        tops.append(
            [p0 + m[2][0] * s[0] + m[2][1] * s[1], p1 + m[3][0] * s[0] + m[3][1] * s[1]]
        )
        if n < count - 1:
            s = [e0 + m[0][0] * s[0] + m[0][1] * s[1], e1 + m[1][0] * s[0] + m[1][1] * s[1]]
    t = [jnp.zeros(shape, F32)] * 2
    for n in range(count - 1, -1, -1):
        m = maps(n)
        keep(n, 1, t)
        if n > 0:
            q0, q1 = tops[n]
            t = [q0 + m[2][2] * t[0] + m[2][3] * t[1], q1 + m[3][2] * t[0] + m[3][3] * t[1]]


def columns_of(block, first, width):
    def one(a, b):
        return jnp.broadcast_to(
            block[6 * a : 6 * a + 6, first + b : first + b + 1], (FIELDS, width)
        )

    return [
        [one(a, b) if a >= 2 or b < 2 else None for b in range(4)] for a in range(4)
    ]


def main_kernel(
    inc_ref,
    res_ref,
    ifac_ref,
    kfac_ref,
    coup_ref,
    cell_ref,
    weight_ref,
    out_ref,
    acc,
    place,
    x,
    i_mat,
    i_state,
    i_ends,
    i_maps,
    i_out,
    i_in,
    s_out,
    s_in,
    k_mat,
    k_state,
    k_ends,
    k_pad,
    k_all,
    k_st,
    xk,
    map_send,
    map_recv,
    end_send,
    end_recv,
    st_send,
    st_recv,
    k_send,
    k_recv,
):
    line, block = lax.axis_index("line"), lax.axis_index("block")
    barrier = pltpu.get_barrier_semaphore()
    for d in range(1, LINES):
        pl.semaphore_signal(
            barrier, inc=1, device_id={"line": (line + d) % LINES}, device_id_type=MESH
        )
    for d in range(1, BLOCKS):
        pl.semaphore_signal(
            barrier, inc=1, device_id={"block": (block + d) % BLOCKS}, device_id_type=MESH
        )
    prepare_i(ifac_ref, coup_ref, i_mat, i_state, i_ends, i_maps.at[line])
    pl.semaphore_wait(barrier, LINES + BLOCKS - 2)

    def to_line(d, src, dst, send, recv):
        return pltpu.make_async_remote_copy(
            src_ref=src,
            dst_ref=dst,
            send_sem=send.at[d],
            recv_sem=recv.at[d],
            device_id={"line": (line + d) % LINES},
            device_id_type=MESH,
        )

    map_copies = [
        to_line(d, i_maps.at[line], i_maps.at[line], map_send, map_recv) for d in range(1, LINES)
    ]
    for copy in map_copies:
        copy.start()
    prepare_k(kfac_ref, coup_ref, k_mat, k_state, k_ends, k_pad)
    scatter_all(inc_ref, cell_ref, weight_ref, acc, place)

    n = FIELDS * CI
    for j in range(CJ):
        total = res_ref[:, j].reshape(n, CK)
        if j < 8:
            total = total + acc[j * n : (j + 1) * n, 0:CK]
        if j >= 7:
            total = total + acc[(j - 7) * n : (j - 6) * n, CK : 2 * CK]
        x[:, j * CK : (j + 1) * CK] = total
    x[:, CJ * CK :] = jnp.zeros((n, CK), F32)

    ends = mm(i_ends[...], x[...])
    for c in range(LINES):
        i_out[c] = ends[:, c * 256 : (c + 1) * 256]
    i_in[line] = i_out[line]
    end_copies = [
        to_line(d, i_out.at[(line + d) % LINES], i_in.at[line], end_send, end_recv)
        for d in range(1, LINES)
    ]
    for copy in end_copies:
        copy.start()
    x[...] = mm(i_mat[...], x[...])
    for copy in map_copies:
        copy.wait()
    for copy in end_copies:
        copy.wait()

    def i_end(s):
        return [i_in[s, 6 * a : 6 * a + 6, :] for a in range(4)]

    i_cols = [columns_of(i_maps[s], 0, 256) for s in range(LINES)]

    def i_keep(s, up, state):
        for a in range(2):
            at = 12 * up + 6 * a
            s_out[s, at : at + 6, :] = state[a]

    chain(LINES, i_end, lambda s: i_cols[s], i_keep)
    s_in[line] = s_out[line]
    st_copies = [
        to_line(d, s_out.at[(line + d) % LINES], s_in.at[line], st_send, st_recv)
        for d in range(1, LINES)
    ]
    for copy in st_copies:
        copy.start()
    for copy in st_copies:
        copy.wait()
    for c in range(LINES):
        part = x[:, c * 256 : (c + 1) * 256] + mm(i_state[...], s_in[c])
        for jj in range(2):
            j = 2 * c + jj
            for f in range(FIELDS):
                xk[f, j * 8 : j * 8 + 8, :] = part[f * 8 : f * 8 + 8, jj * CK : (jj + 1) * CK]

    for f in range(FIELDS):
        found = mm_nt(k_ends[f], xk[f]) + k_pad[f]
        for a in range(4):
            k_all[block, 6 * a + f : 6 * a + f + 1, :] = found[a : a + 1]
    k_copies = [
        pltpu.make_async_remote_copy(
            src_ref=k_all.at[block],
            dst_ref=k_all.at[block],
            send_sem=k_send.at[d],
            recv_sem=k_recv.at[d],
            device_id={"block": (block + d) % BLOCKS},
            device_id_type=MESH,
        )
        for d in range(1, BLOCKS)
    ]
    for copy in k_copies:
        copy.start()
    for f in range(FIELDS):
        xk[f] = mm_nt(xk[f], k_mat[f])
    for copy in k_copies:
        copy.wait()

    def k_end(s):
        return [k_all[s, 6 * a : 6 * a + 6, :] for a in range(4)]

    k_cols = [columns_of(k_all[s], 120, CK) for s in range(BLOCKS)]
    kept = [[jnp.zeros((FIELDS, CK), F32)] * 2 for _ in range(2)]

    def k_keep(s, up, state):
        kept[up] = [jnp.where(block == s, state[a], kept[up][a]) for a in range(2)]

    chain(BLOCKS, k_end, lambda s: k_cols[s], k_keep)
    k_st[...] = jnp.zeros_like(k_st)
    for f in range(FIELDS):
        for a in range(4):
            k_st[f, a : a + 1, :] = kept[a // 2][a % 2][f : f + 1]
    for f in range(FIELDS):
        done = xk[f] + mm_tn(k_st[f], k_state[f])
        out_ref[f] = done[0 : CJ * CI].reshape(CJ, CI, CK)


def main(incoming, residual, i_factors, k_factors, couplings, donor_cell, donor_weight):
    vmem = pl.BlockSpec(memory_space=pltpu.VMEM)
    n = FIELDS * CI
    dma = pltpu.SemaphoreType.DMA
    return pl.pallas_call(
        main_kernel,
        out_shape=jax.ShapeDtypeStruct((FIELDS, CJ, CI, CK), F32),
        in_specs=[vmem] * 4 + [pl.BlockSpec(memory_space=pltpu.SMEM)] + [vmem] * 2,
        out_specs=vmem,
        scratch_shapes=[
            pltpu.VMEM((384, 256), F32),
            pltpu.VMEM((3, BLOCKS, CAP), jnp.int32),
            pltpu.VMEM((n, 16 * CK), F32),
            pltpu.VMEM((n, n), F32),
            pltpu.VMEM((n, 24), F32),
            pltpu.VMEM((24, n), F32),
            pltpu.VMEM((LINES, 24, CK), F32),
            pltpu.VMEM((LINES, 24, 256), F32),
            pltpu.VMEM((LINES, 24, 256), F32),
            pltpu.VMEM((LINES, 24, 256), F32),
            pltpu.VMEM((LINES, 24, 256), F32),
            pltpu.VMEM((FIELDS, CK, CK), F32),
            pltpu.VMEM((FIELDS, 8, CK), F32),
            pltpu.VMEM((FIELDS, 8, CK), F32),
            pltpu.VMEM((FIELDS, 8, CK), F32),
            pltpu.VMEM((BLOCKS, 24, CK), F32),
            pltpu.VMEM((FIELDS, 8, CK), F32),
            pltpu.VMEM((FIELDS, CK, CK), F32),
            dma((LINES,)),
            dma((LINES,)),
            dma((LINES,)),
            dma((LINES,)),
            dma((LINES,)),
            dma((LINES,)),
            dma((BLOCKS,)),
            dma((BLOCKS,)),
        ],
        compiler_params=pltpu.CompilerParams(
            vmem_limit_bytes=56 * 2**20, collective_id=0, has_side_effects=True
        ),
        name="main",
    )(incoming, residual, i_factors, k_factors, couplings, donor_cell, donor_weight)


def per_device(
    residual,
    adjoint,
    i_factors,
    k_factors,
    couplings,
    receptor_cell,
    send_count,
    donor_cell,
    donor_weight,
):
    outgoing = gather(adjoint.transpose(0, 2, 1, 3), receptor_cell[0, 0], send_count[0, 0])
    incoming = lax.all_to_all(outgoing, "block", split_axis=0, concat_axis=0, tiled=True)
    update = main(
        incoming,
        residual.transpose(0, 2, 1, 3),
        i_factors[0],
        k_factors[0],
        couplings[0, 0].transpose(1, 0, 2),
        donor_cell[0, 0],
        donor_weight[0, 0],
    )
    return update.transpose(0, 2, 1, 3)


def solution(mesh):
    return jax.shard_map(
        per_device,
        mesh=mesh,
        in_specs=(
            P(None, "line", None, "block"),
            P(None, "line", None, "block"),
            P("block", None, None, "line", None),
            P("line", None, None, "block", None),
            P("line", "block", None, None, None),
            P("line", "block", None, None),
            P("line", "block", None),
            P("line", "block", None, None),
            P("line", "block", None, None, None),
        ),
        out_specs=P(None, "line", None, "block"),
        check_vma=False,
    )
```

```python
import functools

import jax
import jax.numpy as jnp
from jax import lax
from jax.experimental import pallas as pl
from jax.experimental.pallas import tpu as pltpu
from jax.sharding import PartitionSpec as P

F32, BF = jnp.float32, jnp.bfloat16
FIELDS, CI, CJ, CK, CAP = 6, 8, 15, 128, 2048
HEAD = 5 * CAP // 8
REST = CAP - HEAD
PART = 384 // 16
LINES, BLOCKS = 8, 16
HIGHEST = lax.Precision.HIGHEST
MESH = pl.DeviceIdType.MESH


def iota(shape, axis):
    return lax.broadcasted_iota(jnp.int32, shape, axis)


def split(x):
    high = x.astype(BF)
    return high, (x - high.astype(F32)).astype(BF)


def as_bf(x):
    return x.astype(F32).astype(BF)


def mm(a, b):
    return jnp.dot(a, b, precision=HIGHEST, preferred_element_type=F32)


def mm_nt(a, b):
    return lax.dot_general(
        a, b, (((1,), (1,)), ((), ())), precision=HIGHEST, preferred_element_type=F32
    )


def mm_tn(a, b):
    return lax.dot_general(
        a, b, (((0,), (0,)), ((), ())), precision=HIGHEST, preferred_element_type=F32
    )


def cell_parts(cell):
    ij = cell >> 7
    i = (ij * 137) >> 11
    return i, ij - i * CJ, cell & 127


def gather_table(adj_ref, table):
    for f in range(FIELDS):
        planes = [adj_ref[f, j] for j in range(CJ)] + [jnp.zeros((CI, CK), F32)]
        for half in range(2):
            high, low = split(jnp.concatenate(planes[8 * half : 8 * half + 8], 0))
            row, col = f * 64, half * CK
            table[row : row + 64, col : col + CK] = high
            table[row : row + 64, 256 + col : 256 + col + CK] = low


def gather_slots(table, group_row, slot_row):
    C = group_row.shape[1]
    slot = as_bf(jnp.broadcast_to(slot_row, (16, C)))
    one, zero = jnp.ones((16, C), BF), jnp.zeros((16, C), BF)
    base = iota((16, C), 0)
    hot = [jnp.where(as_bf(base + 16 * n) == slot, one, zero) for n in range(16)]
    hot = jnp.concatenate(hot, 0)
    found = jnp.dot(
        table[...], jnp.concatenate([hot, hot], 0), preferred_element_type=F32
    ).reshape(FIELDS, 64, C)
    mine = iota((64, C), 0) == jnp.broadcast_to(group_row, (64, C))
    return [
        jnp.sum(jnp.where(mine, found[f], 0.0), axis=0, keepdims=True) for f in range(FIELDS)
    ]


def scatter_slots(values, base_i, base_j, base_t, x, y, z):
    C = x.shape[1]

    def wide(row, n):
        return jnp.broadcast_to(row, (n, C))

    at = iota((8, C), 0)

    def hat(base, t):
        base, t = wide(base, 8), wide(t, 8)
        return jnp.where(at == base, 1.0 - t, jnp.where(at == base + 1, t, 0.0))

    wi, wj = hat(base_i, x), hat(base_j, y)
    u = jnp.concatenate([wide(v, 8) * wi for v in values], 0)
    high, low = [], []
    for r in range(8):
        h, l = split(u * wide(wj[r : r + 1], 48))
        high.append(h)
        low.append(l)
    high, low = jnp.concatenate(high, 0), jnp.concatenate(low, 0)
    z = wide(z, 16)
    z1h, z1l = split(z)
    z0h, z0l = split(1.0 - z)
    t = wide(base_t, 16)
    t0, t1 = as_bf(t), as_bf(t + 1)
    zero = jnp.zeros((16, C), BF)
    base = iota((16, C), 0)
    col_h, col_l = [], []
    for n in range(16):
        r = as_bf(base + 16 * n)
        first, second = r == t0, r == t1
        col_h.append(jnp.where(first, z0h, jnp.where(second, z1h, zero)))
        col_l.append(jnp.where(first, z0l, jnp.where(second, z1l, zero)))
    col_h, col_l = jnp.concatenate(col_h, 0), jnp.concatenate(col_l, 0)
    return lax.dot_general(
        jnp.concatenate([high, high, low], 1),
        jnp.concatenate([col_h, col_l, col_h], 1),
        (((1,), (1,)), ((), ())),
        preferred_element_type=F32,
    )


def donor_parts(cell):
    i, j, k = cell_parts(cell)
    upper = jnp.where(j >= 7, 1, 0)
    return i, j - 7 * upper, upper * CK + k


def entries(shape, items):
    rows, cols = iota(shape, 0), iota(shape, 1)
    out = jnp.zeros(shape, F32)
    for r, c, value in items:
        out = jnp.where((rows == r) & (cols == c), value, out)
    return out


def prepare_i(ifac_ref, coup_ref, i_mat, i_state, i_ends, i_maps_own):
    n = FIELDS * CI
    r, c = iota((n, n), 0), iota((n, n), 1)
    same = (r >> 3) == (c >> 3)
    flip = jnp.where(same & ((r & 7) + (c & 7) == 7), 1.0, 0.0)
    spread = jnp.where(iota((CI, n), 0) == (iota((CI, n), 1) & 7), 1.0, 0.0)

    def diagonal(direction):
        flat = ifac_ref[direction].reshape(n, CI)
        return jnp.where(same, mm(flat, spread), 0.0)

    low = diagonal(0)
    up = mm(flip, mm(diagonal(1), flip))
    whole = mm(up, low)
    shape = (n, 24)
    e_low = entries(
        shape,
        [(8 * f, f, coup_ref[0, 0, f]) for f in range(FIELDS)]
        + [(8 * f, 6 + f, coup_ref[1, 0, f]) for f in range(FIELDS)]
        + [(8 * f + 1, f, coup_ref[2, 0, f]) for f in range(FIELDS)],
    )
    e_up = entries(
        shape,
        [(8 * f + 7, 12 + f, coup_ref[0, 1, f]) for f in range(FIELDS)]
        + [(8 * f + 7, 18 + f, coup_ref[1, 1, f]) for f in range(FIELDS)]
        + [(8 * f + 6, 12 + f, coup_ref[2, 1, f]) for f in range(FIELDS)],
    )
    infl_low = mm(low, e_low)
    state = -mm(up, infl_low + e_up)
    sel_shape = (24, n)
    comp = [(a, f) for a in range(2) for f in range(FIELDS)]
    sel_e = entries(sel_shape, [(a * 6 + f, 8 * f + 7 - a, 1.0) for a, f in comp])
    sel_p = entries(sel_shape, [(12 + a * 6 + f, 8 * f + a, 1.0) for a, f in comp])
    i_mat[...] = whole
    i_state[...] = state
    i_ends[...] = mm(sel_e, low) + mm(sel_p, whole)
    between = mm(sel_p, state) - mm(sel_e, infl_low)
    fold_r, fold_c = iota((24, CK), 0), iota((24, CK), 1)
    fold = jnp.where((fold_r >= 6 * fold_c) & (fold_r < 6 * fold_c + 6), 1.0, 0.0)
    i_maps_own[...] = mm(between, fold)


def stack3(x, axis, middle_low):
    high, low = split(x)
    return jnp.concatenate([high, low, high] if middle_low else [high, high, low], axis)


def mm3(a, b):
    return jnp.dot(stack3(a, 1, False), stack3(b, 0, True), preferred_element_type=F32)


def nt(a, b):
    return lax.dot_general(a, b, (((1,), (1,)), ((), ())), preferred_element_type=F32)


def mm3_nt(a, b):
    return nt(stack3(a, 1, False), stack3(b, 1, True))


def prepare_k(fields, kfac_ref, coup_ref, k_mat, k_state, k_ends, k_pad):
    n = CK
    flip = jnp.where(iota((n, n), 0) + iota((n, n), 1) == n - 1, 1.0, 0.0).astype(BF)
    flip_cols = jnp.concatenate([flip, flip], 0)
    flip_rows = jnp.concatenate([flip, flip], 1)
    sel_e = entries((8, n), [(0, n - 1, 1.0), (1, n - 2, 1.0)])
    sel_p = entries((8, n), [(2, 0, 1.0), (3, 1, 1.0)])
    pad = jnp.zeros((n - 8, n), F32)
    for f in fields:
        low = kfac_ref[0, f]
        up = jnp.dot(
            jnp.concatenate(split(kfac_ref[1, f]), 1), flip_cols, preferred_element_type=F32
        )
        up = jnp.dot(flip_rows, jnp.concatenate(split(up), 0), preferred_element_type=F32)
        whole = mm3(up, low)
        e_low = entries(
            (8, n),
            [(0, 0, coup_ref[0, 2, f]), (0, 1, coup_ref[2, 2, f]), (1, 0, coup_ref[1, 2, f])],
        )
        e_up = entries(
            (8, n),
            [
                (2, n - 1, coup_ref[0, 3, f]),
                (2, n - 2, coup_ref[2, 3, f]),
                (3, n - 1, coup_ref[1, 3, f]),
            ],
        )
        infl_low = mm3_nt(e_low, low)
        state = -mm3_nt(infl_low + e_up, up)
        k_mat[f] = stack3(whole, 1, True)
        k_state[f] = state
        k_ends[f] = stack3(
            jnp.concatenate([low[n - 1 : n], low[n - 2 : n - 1], whole[0:2], pad[0:4]], 0), 1, False
        )
        k_pad[f] = mm3_nt(sel_p, jnp.concatenate([pad, state], 0)) - mm3_nt(
            sel_e, jnp.concatenate([pad, infl_low], 0)
        )


def chain(count, ends, maps, keep):
    shape = ends(0)[0].shape
    s = [jnp.zeros(shape, F32)] * 2
    tops = []
    for n in range(count):
        e0, e1, p0, p1 = ends(n)
        m = maps(n)
        keep(n, 0, s)
        tops.append(
            [p0 + m[2][0] * s[0] + m[2][1] * s[1], p1 + m[3][0] * s[0] + m[3][1] * s[1]]
        )
        if n < count - 1:
            s = [e0 + m[0][0] * s[0] + m[0][1] * s[1], e1 + m[1][0] * s[0] + m[1][1] * s[1]]
    t = [jnp.zeros(shape, F32)] * 2
    for n in range(count - 1, -1, -1):
        m = maps(n)
        keep(n, 1, t)
        if n > 0:
            q0, q1 = tops[n]
            t = [q0 + m[2][2] * t[0] + m[2][3] * t[1], q1 + m[3][2] * t[0] + m[3][3] * t[1]]


def columns_of(block, first, width):
    def one(a, b):
        return jnp.broadcast_to(
            block[6 * a : 6 * a + 6, first + b : first + b + 1], (FIELDS, width)
        )

    return [
        [one(a, b) if a >= 2 or b < 2 else None for b in range(4)] for a in range(4)
    ]


def main_kernel(
    adj_ref,
    rec_ref,
    res_ref,
    ifac_ref,
    kfac_ref,
    coup_ref,
    count_ref,
    cell_ref,
    weight_ref,
    out_ref,
    table,
    where_ref,
    place,
    outgoing,
    incoming,
    info_out,
    info_in,
    acc,
    acc_rest,
    rs_in,
    ag_in,
    x,
    i_mat,
    i_state,
    i_ends,
    i_maps,
    i_out,
    i_in,
    s_out,
    s_in,
    k_mat,
    k_state,
    k_ends,
    k_pad,
    k_all,
    k_st,
    xk,
    info_send,
    info_recv,
    a2a_send,
    a2a_recv,
    rs_send,
    rs_recv,
    ag_send,
    ag_recv,
    map_send,
    map_recv,
    end_send,
    end_recv,
    st_send,
    st_recv,
    k_send,
    k_recv,
):
    line, block = lax.axis_index("line"), lax.axis_index("block")
    barrier = pltpu.get_barrier_semaphore()
    for d in range(1, LINES):
        pl.semaphore_signal(
            barrier, inc=1, device_id={"line": lax.rem(line + d, LINES)}, device_id_type=MESH
        )
    for d in range(1, BLOCKS):
        pl.semaphore_signal(
            barrier, inc=1, device_id={"block": lax.rem(block + d, BLOCKS)}, device_id_type=MESH
        )

    def to_line(d, src, dst, send, recv):
        return pltpu.make_async_remote_copy(
            src_ref=src,
            dst_ref=dst,
            send_sem=send.at[d],
            recv_sem=recv.at[d],
            device_id={"line": lax.rem(line + d, LINES)},
            device_id_type=MESH,
        )

    def to_block(d, src, dst, send, recv):
        return pltpu.make_async_remote_copy(
            src_ref=src,
            dst_ref=dst,
            send_sem=send.at[d],
            recv_sem=recv.at[d],
            device_id={"block": lax.rem(block + d, BLOCKS)},
            device_id_type=MESH,
        )

    def peer(d):
        return lax.rem(block + d, BLOCKS)

    def info_copy(d):
        return to_block(d, info_out.at[peer(d)], info_in.at[block], info_send, info_recv)

    def slot_copy(d):
        return to_block(d, outgoing.at[peer(d)], incoming.at[block], a2a_send, a2a_recv)

    def rs_copy(d):
        return to_block(d, acc_rest.at[peer(d)], rs_in.at[block], rs_send, rs_recv)

    def ag_copy(d):
        return to_block(d, ag_in.at[block], ag_in.at[block], ag_send, ag_recv)

    def over_peers(action):
        def step(d, carry):
            action(d)
            return carry

        lax.fori_loop(1, BLOCKS, step, 0)

    hot = jnp.int32(0)
    for o in range(BLOCKS):
        hot = jnp.where(count_ref[o] == CAP, o, hot)

    for p in range(BLOCKS):
        info_out[p, 0:1, :] = cell_ref[p : p + 1, HEAD:].astype(F32)
        for a in range(3):
            info_out[p, a + 1 : a + 2, :] = weight_ref[a, p : p + 1, HEAD:]
    gather_table(adj_ref, table)
    i, j, k = cell_parts(rec_ref[...])
    where_ref[0] = (j & 7) * CI + i
    where_ref[1] = (j >> 3) * CK + k
    for a, part in enumerate(donor_parts(cell_ref[...])):
        place[a] = part
    prepare_i(ifac_ref, coup_ref, i_mat, i_state, i_ends, i_maps.at[line])
    pl.semaphore_wait(barrier, LINES + BLOCKS - 2)
    over_peers(lambda d: info_copy(d).start())
    info_in[block] = info_out[block]

    def owner_step(d, carry):
        o = peer(d)
        rows = gather_slots(
            table, where_ref[0, pl.ds(o, 1), 0:HEAD], where_ref[1, pl.ds(o, 1), 0:HEAD]
        )
        live = iota((1, HEAD), 1) < count_ref[o]
        for f in range(FIELDS):
            outgoing[o, f : f + 1, :] = jnp.where(live, rows[f], 0.0)

        @pl.when(d < BLOCKS)
        def _():
            slot_copy(d).start()

        return carry

    lax.fori_loop(1, BLOCKS + 1, owner_step, 0)
    incoming[block] = outgoing[block]
    map_copies = [
        to_line(d, i_maps.at[line], i_maps.at[line], map_send, map_recv) for d in range(1, LINES)
    ]
    for copy in map_copies:
        copy.start()

    over_peers(lambda d: info_copy(d).wait())
    rest = gather_slots(
        table, where_ref[0, pl.ds(hot, 1), HEAD:], where_ref[1, pl.ds(hot, 1), HEAD:]
    )
    info = info_in[hot]
    found = scatter_slots(
        rest,
        *donor_parts(info[0:1].astype(jnp.int32)),
        info[1:2],
        info[2:3],
        info[3:4],
    )
    for p in range(BLOCKS):
        acc_rest[p] = found[p * PART : (p + 1) * PART]
    rs_in[block] = acc_rest[block]
    over_peers(lambda d: rs_copy(d).start())

    acc[...] = jnp.zeros_like(acc)

    def source_step(d, carry):
        s = lax.rem(block + BLOCKS - d, BLOCKS)

        @pl.when(d > 0)
        def _():
            slot_copy(d).wait_recv()

        @pl.when(d == BLOCKS // 2)
        def _():
            over_peers(lambda e: rs_copy(e).wait())
            total = rs_in[0]
            for p in range(1, BLOCKS):
                total = total + rs_in[p]
            ag_in[block] = total
            over_peers(lambda e: ag_copy(e).start())

        def row(ref, a):
            return ref[a, pl.ds(s, 1), 0:HEAD]

        values = incoming[s]
        acc[...] += scatter_slots(
            [values[f : f + 1] for f in range(FIELDS)],
            *[row(place, a) for a in range(3)],
            *[row(weight_ref, a) for a in range(3)],
        )
        return carry

    lax.fori_loop(0, BLOCKS, source_step, 0)
    over_peers(lambda d: slot_copy(d).wait_send())
    over_peers(lambda d: ag_copy(d).wait())

    n = FIELDS * CI
    for j in range(CJ):
        total = res_ref[:, j].reshape(n, CK)
        for r, c in ((j, 0), (j - 7, CK)):
            if 0 <= r < 8:
                more = jnp.concatenate([ag_in[2 * r, :, c : c + CK], ag_in[2 * r + 1, :, c : c + CK]], 0)
                more = jnp.where(hot == block, more, 0.0)
                total = total + acc[r * n : (r + 1) * n, c : c + CK] + more
        x[:, j * CK : (j + 1) * CK] = total
    x[:, CJ * CK :] = jnp.zeros((n, CK), F32)

    ends = mm(i_ends[...], x[...])
    for c in range(LINES):
        i_out[c] = ends[:, c * 256 : (c + 1) * 256]
    i_in[line] = i_out[line]
    end_copies = [
        to_line(d, i_out.at[(line + d) % LINES], i_in.at[line], end_send, end_recv)
        for d in range(1, LINES)
    ]
    for copy in end_copies:
        copy.start()
    x[...] = mm(i_mat[...], x[...])
    k_refs = (kfac_ref, coup_ref, k_mat, k_state, k_ends, k_pad)
    prepare_k(range(0, 3), *k_refs)
    for copy in map_copies:
        copy.wait()
    for copy in end_copies:
        copy.wait()

    def i_end(s):
        return [i_in[s, 6 * a : 6 * a + 6, :] for a in range(4)]

    i_cols = [columns_of(i_maps[s], 0, 256) for s in range(LINES)]

    def i_keep(s, up, state):
        for a in range(2):
            at = 12 * up + 6 * a
            s_out[s, at : at + 6, :] = state[a]

    chain(LINES, i_end, lambda s: i_cols[s], i_keep)
    s_in[line] = s_out[line]
    st_copies = [
        to_line(d, s_out.at[(line + d) % LINES], s_in.at[line], st_send, st_recv)
        for d in range(1, LINES)
    ]
    for copy in st_copies:
        copy.start()
    prepare_k(range(3, 6), *k_refs)
    for copy in st_copies:
        copy.wait()
    for c in range(LINES):
        part = x[:, c * 256 : (c + 1) * 256] + mm(i_state[...], s_in[c])
        for jj in range(2):
            j = 2 * c + jj
            for f in range(FIELDS):
                xk[f, j * 8 : j * 8 + 8, :] = part[f * 8 : f * 8 + 8, jj * CK : (jj + 1) * CK]

    for f in range(FIELDS):
        found = nt(k_ends[f], stack3(xk[f], 1, True)) + k_pad[f]
        for a in range(4):
            k_all[block, 6 * a + f : 6 * a + f + 1, :] = found[a : a + 1]
    k_copies = [
        pltpu.make_async_remote_copy(
            src_ref=k_all.at[block],
            dst_ref=k_all.at[block],
            send_sem=k_send.at[d],
            recv_sem=k_recv.at[d],
            device_id={"block": (block + d) % BLOCKS},
            device_id_type=MESH,
        )
        for d in range(1, BLOCKS)
    ]
    for copy in k_copies:
        copy.start()
    for f in range(FIELDS):
        xk[f] = nt(stack3(xk[f], 1, False), k_mat[f])
    for copy in k_copies:
        copy.wait()

    def k_end(s):
        return [k_all[s, 6 * a : 6 * a + 6, :] for a in range(4)]

    k_cols = [columns_of(k_all[s], 120, CK) for s in range(BLOCKS)]
    kept = [[jnp.zeros((FIELDS, CK), F32)] * 2 for _ in range(2)]

    def k_keep(s, up, state):
        kept[up] = [jnp.where(block == s, state[a], kept[up][a]) for a in range(2)]

    chain(BLOCKS, k_end, lambda s: k_cols[s], k_keep)
    k_st[...] = jnp.zeros_like(k_st)
    for f in range(FIELDS):
        for a in range(4):
            k_st[f, a : a + 1, :] = kept[a // 2][a % 2][f : f + 1]
    for f in range(FIELDS):
        done = xk[f] + mm_tn(k_st[f], k_state[f])
        out_ref[f] = done[0 : CJ * CI].reshape(CJ, CI, CK)


def sweep(
    adjoint,
    receptor_cell,
    residual,
    i_factors,
    k_factors,
    couplings,
    send_count,
    donor_cell,
    donor_weight,
):
    vmem, smem = pl.BlockSpec(memory_space=pltpu.VMEM), pl.BlockSpec(memory_space=pltpu.SMEM)
    n = FIELDS * CI
    dma = pltpu.SemaphoreType.DMA
    return pl.pallas_call(
        main_kernel,
        out_shape=jax.ShapeDtypeStruct((FIELDS, CJ, CI, CK), F32),
        in_specs=[vmem] * 5 + [smem] * 2 + [vmem] * 2,
        out_specs=vmem,
        scratch_shapes=[
            pltpu.VMEM((FIELDS * 64, 512), BF),
            pltpu.VMEM((2, BLOCKS, CAP), jnp.int32),
            pltpu.VMEM((3, BLOCKS, CAP), jnp.int32),
            pltpu.VMEM((BLOCKS, FIELDS, HEAD), F32),
            pltpu.VMEM((BLOCKS, FIELDS, HEAD), F32),
            pltpu.VMEM((BLOCKS, 4, REST), F32),
            pltpu.VMEM((BLOCKS, 4, REST), F32),
            pltpu.VMEM((384, 256), F32),
            pltpu.VMEM((BLOCKS, PART, 256), F32),
            pltpu.VMEM((BLOCKS, PART, 256), F32),
            pltpu.VMEM((BLOCKS, PART, 256), F32),
            pltpu.VMEM((n, 16 * CK), F32),
            pltpu.VMEM((n, n), F32),
            pltpu.VMEM((n, 24), F32),
            pltpu.VMEM((24, n), F32),
            pltpu.VMEM((LINES, 24, CK), F32),
            pltpu.VMEM((LINES, 24, 256), F32),
            pltpu.VMEM((LINES, 24, 256), F32),
            pltpu.VMEM((LINES, 24, 256), F32),
            pltpu.VMEM((LINES, 24, 256), F32),
            pltpu.VMEM((FIELDS, CK, 3 * CK), BF),
            pltpu.VMEM((FIELDS, 8, CK), F32),
            pltpu.VMEM((FIELDS, 8, 3 * CK), BF),
            pltpu.VMEM((FIELDS, 8, CK), F32),
            pltpu.VMEM((BLOCKS, 24, CK), F32),
            pltpu.VMEM((FIELDS, 8, CK), F32),
            pltpu.VMEM((FIELDS, CK, CK), F32),
        ]
        + [dma((BLOCKS,))] * 8
        + [dma((LINES,))] * 6
        + [dma((BLOCKS,))] * 2,
        compiler_params=pltpu.CompilerParams(
            vmem_limit_bytes=56 * 2**20, collective_id=0, has_side_effects=True
        ),
        name="sweep",
    )(
        adjoint,
        receptor_cell,
        residual,
        i_factors,
        k_factors,
        couplings,
        send_count,
        donor_cell,
        donor_weight,
    )


def per_device(
    residual,
    adjoint,
    i_factors,
    k_factors,
    couplings,
    receptor_cell,
    send_count,
    donor_cell,
    donor_weight,
):
    update = sweep(
        adjoint.transpose(0, 2, 1, 3),
        receptor_cell[0, 0],
        residual.transpose(0, 2, 1, 3),
        i_factors[0],
        k_factors[0],
        couplings[0, 0].transpose(1, 0, 2),
        send_count[0, 0],
        donor_cell[0, 0],
        donor_weight[0, 0],
    )
    return update.transpose(0, 2, 1, 3)


def solution(mesh):
    return jax.shard_map(
        per_device,
        mesh=mesh,
        in_specs=(
            P(None, "line", None, "block"),
            P(None, "line", None, "block"),
            P("block", None, None, "line", None),
            P("line", None, None, "block", None),
            P("line", "block", None, None, None),
            P("line", "block", None, None),
            P("line", "block", None),
            P("line", "block", None, None),
            P("line", "block", None, None, None),
        ),
        out_specs=P(None, "line", None, "block"),
        check_vma=False,
    )
```

```python
import functools

import jax
import jax.numpy as jnp
from jax import lax
from jax.experimental import pallas as pl
from jax.experimental.pallas import tpu as pltpu
from jax.sharding import PartitionSpec as P

F32, BF = jnp.float32, jnp.bfloat16
FIELDS, CI, CJ, CK, CAP = 6, 8, 15, 128, 2048
HEAD = 5 * CAP // 8
REST = CAP - HEAD
PART = 384 // 16
PIECES = HEAD // 256
EARLY = 1
LINES, BLOCKS = 8, 16
HIGHEST = lax.Precision.HIGHEST
MESH = pl.DeviceIdType.MESH


def iota(shape, axis):
    return lax.broadcasted_iota(jnp.int32, shape, axis)


def split(x):
    high = x.astype(BF)
    return high, (x - high.astype(F32)).astype(BF)


def as_bf(x):
    return x.astype(F32).astype(BF)


def mm(a, b):
    return jnp.dot(a, b, precision=HIGHEST, preferred_element_type=F32)


def mm_nt(a, b):
    return lax.dot_general(
        a, b, (((1,), (1,)), ((), ())), precision=HIGHEST, preferred_element_type=F32
    )


def mm_tn(a, b):
    return lax.dot_general(
        a, b, (((0,), (0,)), ((), ())), precision=HIGHEST, preferred_element_type=F32
    )


def cell_parts(cell):
    ij = cell >> 7
    i = (ij * 137) >> 11
    return i, ij - i * CJ, cell & 127


def gather_table(adj_ref, table):
    for f in range(FIELDS):
        planes = [adj_ref[f, j] for j in range(CJ)] + [jnp.zeros((CI, CK), F32)]
        for half in range(2):
            high, low = split(jnp.concatenate(planes[8 * half : 8 * half + 8], 0))
            row, col = f * 64, half * CK
            table[row : row + 64, col : col + CK] = high
            table[row : row + 64, 256 + col : 256 + col + CK] = low


def gather_slots(table, group_row, slot_row):
    C = group_row.shape[1]
    slot = as_bf(jnp.broadcast_to(slot_row, (16, C)))
    one, zero = jnp.ones((16, C), BF), jnp.zeros((16, C), BF)
    base = iota((16, C), 0)
    hot = [jnp.where(as_bf(base + 16 * n) == slot, one, zero) for n in range(16)]
    hot = jnp.concatenate(hot, 0)
    found = jnp.dot(
        table[...], jnp.concatenate([hot, hot], 0), preferred_element_type=F32
    ).reshape(FIELDS, 64, C)
    mine = iota((64, C), 0) == jnp.broadcast_to(group_row, (64, C))
    return [
        jnp.sum(jnp.where(mine, found[f], 0.0), axis=0, keepdims=True) for f in range(FIELDS)
    ]


def scatter_slots(values, base_i, base_j, base_t, x, y, z):
    C = x.shape[1]

    def wide(row, n):
        return jnp.broadcast_to(row, (n, C))

    at = iota((8, C), 0)

    def hat(base, t):
        base, t = wide(base, 8), wide(t, 8)
        return jnp.where(at == base, 1.0 - t, jnp.where(at == base + 1, t, 0.0))

    wi, wj = hat(base_i, x), hat(base_j, y)
    u = jnp.concatenate([wide(v, 8) * wi for v in values], 0)
    high, low = [], []
    for r in range(8):
        h, l = split(u * wide(wj[r : r + 1], 48))
        high.append(h)
        low.append(l)
    high, low = jnp.concatenate(high, 0), jnp.concatenate(low, 0)
    z = wide(z, 16)
    z1h, z1l = split(z)
    z0h, z0l = split(1.0 - z)
    t = wide(base_t, 16)
    t0, t1 = as_bf(t), as_bf(t + 1)
    zero = jnp.zeros((16, C), BF)
    base = iota((16, C), 0)
    col_h, col_l = [], []
    for n in range(16):
        r = as_bf(base + 16 * n)
        first, second = r == t0, r == t1
        col_h.append(jnp.where(first, z0h, jnp.where(second, z1h, zero)))
        col_l.append(jnp.where(first, z0l, jnp.where(second, z1l, zero)))
    col_h, col_l = jnp.concatenate(col_h, 0), jnp.concatenate(col_l, 0)
    return lax.dot_general(
        jnp.concatenate([high, high, low], 1),
        jnp.concatenate([col_h, col_l, col_h], 1),
        (((1,), (1,)), ((), ())),
        preferred_element_type=F32,
    )


def donor_parts(cell):
    i, j, k = cell_parts(cell)
    upper = jnp.where(j >= 7, 1, 0)
    return i, j - 7 * upper, upper * CK + k


def entries(shape, items):
    rows, cols = iota(shape, 0), iota(shape, 1)
    out = jnp.zeros(shape, F32)
    for r, c, value in items:
        out = jnp.where((rows == r) & (cols == c), value, out)
    return out


def prepare_i(ifac_ref, coup_ref, i_mat, i_state, i_ends, i_maps_own):
    n = FIELDS * CI
    r, c = iota((n, n), 0), iota((n, n), 1)
    same = (r >> 3) == (c >> 3)
    flip = jnp.where(same & ((r & 7) + (c & 7) == 7), 1.0, 0.0)
    spread = jnp.where(iota((CI, n), 0) == (iota((CI, n), 1) & 7), 1.0, 0.0)

    def diagonal(direction):
        flat = ifac_ref[direction].reshape(n, CI)
        return jnp.where(same, mm(flat, spread), 0.0)

    low = diagonal(0)
    up = mm(flip, mm(diagonal(1), flip))
    whole = mm(up, low)
    shape = (n, 24)
    e_low = entries(
        shape,
        [(8 * f, f, coup_ref[0, 0, f]) for f in range(FIELDS)]
        + [(8 * f, 6 + f, coup_ref[1, 0, f]) for f in range(FIELDS)]
        + [(8 * f + 1, f, coup_ref[2, 0, f]) for f in range(FIELDS)],
    )
    e_up = entries(
        shape,
        [(8 * f + 7, 12 + f, coup_ref[0, 1, f]) for f in range(FIELDS)]
        + [(8 * f + 7, 18 + f, coup_ref[1, 1, f]) for f in range(FIELDS)]
        + [(8 * f + 6, 12 + f, coup_ref[2, 1, f]) for f in range(FIELDS)],
    )
    infl_low = mm(low, e_low)
    state = -mm(up, infl_low + e_up)
    sel_shape = (24, n)
    comp = [(a, f) for a in range(2) for f in range(FIELDS)]
    sel_e = entries(sel_shape, [(a * 6 + f, 8 * f + 7 - a, 1.0) for a, f in comp])
    sel_p = entries(sel_shape, [(12 + a * 6 + f, 8 * f + a, 1.0) for a, f in comp])
    i_mat[...] = whole
    i_state[...] = state
    i_ends[...] = mm(sel_e, low) + mm(sel_p, whole)
    between = mm(sel_p, state) - mm(sel_e, infl_low)
    fold_r, fold_c = iota((24, CK), 0), iota((24, CK), 1)
    fold = jnp.where((fold_r >= 6 * fold_c) & (fold_r < 6 * fold_c + 6), 1.0, 0.0)
    i_maps_own[...] = mm(between, fold)


def stack3(x, axis, middle_low):
    high, low = split(x)
    return jnp.concatenate([high, low, high] if middle_low else [high, high, low], axis)


def mm3(a, b):
    return jnp.dot(stack3(a, 1, False), stack3(b, 0, True), preferred_element_type=F32)


def nt(a, b):
    return lax.dot_general(a, b, (((1,), (1,)), ((), ())), preferred_element_type=F32)


def mm3_nt(a, b):
    return nt(stack3(a, 1, False), stack3(b, 1, True))


def prepare_k(fields, kfac_ref, coup_ref, k_mat, k_state, k_ends, k_pad):
    n = CK
    flip = jnp.where(iota((n, n), 0) + iota((n, n), 1) == n - 1, 1.0, 0.0).astype(BF)
    flip_cols = jnp.concatenate([flip, flip], 0)
    flip_rows = jnp.concatenate([flip, flip], 1)
    sel_e = entries((8, n), [(0, n - 1, 1.0), (1, n - 2, 1.0)])
    sel_p = entries((8, n), [(2, 0, 1.0), (3, 1, 1.0)])
    pad = jnp.zeros((n - 8, n), F32)
    for f in fields:
        low = kfac_ref[0, f]
        up = jnp.dot(
            jnp.concatenate(split(kfac_ref[1, f]), 1), flip_cols, preferred_element_type=F32
        )
        up = jnp.dot(flip_rows, jnp.concatenate(split(up), 0), preferred_element_type=F32)
        whole = mm3(up, low)
        e_low = entries(
            (8, n),
            [(0, 0, coup_ref[0, 2, f]), (0, 1, coup_ref[2, 2, f]), (1, 0, coup_ref[1, 2, f])],
        )
        e_up = entries(
            (8, n),
            [
                (2, n - 1, coup_ref[0, 3, f]),
                (2, n - 2, coup_ref[2, 3, f]),
                (3, n - 1, coup_ref[1, 3, f]),
            ],
        )
        infl_low = mm3_nt(e_low, low)
        state = -mm3_nt(infl_low + e_up, up)
        k_mat[f] = stack3(whole, 1, True)
        k_state[f] = state
        k_ends[f] = stack3(
            jnp.concatenate([low[n - 1 : n], low[n - 2 : n - 1], whole[0:2], pad[0:4]], 0), 1, False
        )
        k_pad[f] = mm3_nt(sel_p, jnp.concatenate([pad, state], 0)) - mm3_nt(
            sel_e, jnp.concatenate([pad, infl_low], 0)
        )


def chain(count, ends, maps, keep):
    shape = ends(0)[0].shape
    s = [jnp.zeros(shape, F32)] * 2
    tops = []
    for n in range(count):
        e0, e1, p0, p1 = ends(n)
        m = maps(n)
        keep(n, 0, s)
        tops.append(
            [p0 + m[2][0] * s[0] + m[2][1] * s[1], p1 + m[3][0] * s[0] + m[3][1] * s[1]]
        )
        if n < count - 1:
            s = [e0 + m[0][0] * s[0] + m[0][1] * s[1], e1 + m[1][0] * s[0] + m[1][1] * s[1]]
    t = [jnp.zeros(shape, F32)] * 2
    for n in range(count - 1, -1, -1):
        m = maps(n)
        keep(n, 1, t)
        if n > 0:
            q0, q1 = tops[n]
            t = [q0 + m[2][2] * t[0] + m[2][3] * t[1], q1 + m[3][2] * t[0] + m[3][3] * t[1]]


def columns_of(block, first, width):
    def one(a, b):
        return jnp.broadcast_to(
            block[6 * a : 6 * a + 6, first + b : first + b + 1], (FIELDS, width)
        )

    return [
        [one(a, b) if a >= 2 or b < 2 else None for b in range(4)] for a in range(4)
    ]


def main_kernel(
    adj_ref,
    rec_ref,
    res_hbm,
    ifac_ref,
    kfac_hbm,
    coup_ref,
    count_ref,
    cell_ref,
    weight_ref,
    out_ref,
    table,
    where_ref,
    place,
    outgoing,
    incoming,
    info_out,
    info_in,
    rest,
    acc,
    acc_rest,
    rs_in,
    ag_in,
    x,
    i_mat,
    i_state,
    i_ends,
    i_maps,
    i_out,
    i_in,
    s_out,
    s_in,
    k_mat,
    k_state,
    k_ends,
    k_pad,
    k_all,
    k_st,
    xk,
    info_send,
    info_recv,
    a2a_send,
    a2a_recv,
    rs_send,
    rs_recv,
    ag_send,
    ag_recv,
    map_send,
    map_recv,
    end_send,
    end_recv,
    st_send,
    st_recv,
    k_send,
    k_recv,
    res_ref,
    kfac_ref,
    load_sem,
):
    load_res = pltpu.make_async_copy(res_hbm, res_ref, load_sem.at[0])
    load_kfac = pltpu.make_async_copy(kfac_hbm, kfac_ref, load_sem.at[1])
    load_res.start()
    load_kfac.start()
    line, block = lax.axis_index("line"), lax.axis_index("block")
    barrier = pltpu.get_barrier_semaphore()
    for d in range(1, LINES):
        pl.semaphore_signal(
            barrier, inc=1, device_id={"line": lax.rem(line + d, LINES)}, device_id_type=MESH
        )
    for d in range(1, BLOCKS):
        pl.semaphore_signal(
            barrier, inc=1, device_id={"block": lax.rem(block + d, BLOCKS)}, device_id_type=MESH
        )

    def to_line(d, src, dst, send, recv):
        return pltpu.make_async_remote_copy(
            src_ref=src,
            dst_ref=dst,
            send_sem=send.at[d],
            recv_sem=recv.at[d],
            device_id={"line": lax.rem(line + d, LINES)},
            device_id_type=MESH,
        )

    def to_block(d, src, dst, send, recv):
        return pltpu.make_async_remote_copy(
            src_ref=src,
            dst_ref=dst,
            send_sem=send.at[d],
            recv_sem=recv.at[d],
            device_id={"block": lax.rem(block + d, BLOCKS)},
            device_id_type=MESH,
        )

    def peer(d):
        return lax.rem(block + d, BLOCKS)

    def info_copy(d):
        return to_block(d, info_out.at[peer(d)], info_in.at[block], info_send, info_recv)

    def slot_copy(d):
        return to_block(d, outgoing.at[peer(d)], incoming.at[block], a2a_send, a2a_recv)

    def rs_copy(d):
        return to_block(d, acc_rest.at[peer(d)], rs_in.at[block], rs_send, rs_recv)

    def ag_copy(d):
        return to_block(d, ag_in.at[block], ag_in.at[block], ag_send, ag_recv)

    def over_peers(action):
        def step(d, carry):
            action(d)
            return carry

        lax.fori_loop(1, BLOCKS, step, 0)

    hot = jnp.int32(0)
    for o in range(BLOCKS):
        hot = jnp.where(count_ref[o] == CAP, o, hot)

    for p in range(BLOCKS):
        info_out[p, 0:1, :] = cell_ref[p : p + 1, HEAD:].astype(F32)
        for a in range(3):
            info_out[p, a + 1 : a + 2, :] = weight_ref[a, p : p + 1, HEAD:]
    gather_table(adj_ref, table)
    i, j, k = cell_parts(rec_ref[...])
    where_ref[0] = (j & 7) * CI + i
    where_ref[1] = (j >> 3) * CK + k
    for a, part in enumerate(donor_parts(cell_ref[...])):
        place[a] = part
    prepare_i(ifac_ref, coup_ref, i_mat, i_state, i_ends, i_maps.at[line])
    outgoing[:, FIELDS * PIECES :, :] = jnp.zeros((BLOCKS, 32 - FIELDS * PIECES, 256), F32)

    def owner_step(t, carry):
        owners = [peer(2 * t), peer(2 * t + 1)]
        group_row, slot_row = [
            jnp.concatenate([where_ref[a, pl.ds(o, 1), 0:HEAD] for o in owners], 1)
            for a in range(2)
        ]
        rows = gather_slots(table, group_row, slot_row)
        for n, o in enumerate(owners):
            live = iota((1, HEAD), 1) < count_ref[o]
            for f in range(FIELDS):
                row = jnp.where(live, rows[f][:, n * HEAD : (n + 1) * HEAD], 0.0)
                for q in range(PIECES):
                    at = q * FIELDS + f
                    outgoing[o, at : at + 1, :] = row[:, q * 256 : (q + 1) * 256]
        return carry

    lax.fori_loop(0, EARLY, owner_step, 0)
    incoming[block] = outgoing[block]
    for f, row in enumerate(
        gather_slots(table, where_ref[0, pl.ds(hot, 1), HEAD:], where_ref[1, pl.ds(hot, 1), HEAD:])
    ):
        rest[f : f + 1, :] = row

    pl.semaphore_wait(barrier, LINES + BLOCKS - 2)
    over_peers(lambda d: info_copy(d).start())

    def early_step(d, carry):
        slot_copy(d).start()
        return carry

    lax.fori_loop(1, 2 * EARLY, early_step, 0)
    map_copies = [
        to_line(d, i_maps.at[line], i_maps.at[line], map_send, map_recv) for d in range(1, LINES)
    ]
    for copy in map_copies:
        copy.start()
    info_in[block] = info_out[block]

    def late_step(d, carry):
        owner_step(d, carry)
        slot_copy(2 * d).start()
        slot_copy(2 * d + 1).start()
        return carry

    lax.fori_loop(EARLY, BLOCKS // 2, late_step, 0)

    over_peers(lambda d: info_copy(d).wait())
    info = info_in[hot]
    found = scatter_slots(
        [rest[f : f + 1, :] for f in range(FIELDS)],
        *donor_parts(info[0:1].astype(jnp.int32)),
        info[1:2],
        info[2:3],
        info[3:4],
    )
    for p in range(BLOCKS):
        acc_rest[p] = found[p * PART : (p + 1) * PART]
    rs_in[block] = acc_rest[block]
    over_peers(lambda d: rs_copy(d).start())

    acc[...] = jnp.zeros_like(acc)

    def source_step(t, carry):
        sources = [lax.rem(block + BLOCKS - 2 * t - n, BLOCKS) for n in range(2)]

        @pl.when(t > 0)
        def _():
            slot_copy(2 * t).wait_recv()

        slot_copy(2 * t + 1).wait_recv()

        @pl.when(t == BLOCKS // 4)
        def _():
            over_peers(lambda e: rs_copy(e).wait())
            total = rs_in[0]
            for p in range(1, BLOCKS):
                total = total + rs_in[p]
            ag_in[block] = total
            over_peers(lambda e: ag_copy(e).start())

        def row(ref, a):
            return jnp.concatenate([ref[a, pl.ds(s, 1), 0:HEAD] for s in sources], 1)

        values = [incoming[s] for s in sources]
        acc[...] += scatter_slots(
            [
                jnp.concatenate(
                    [v[q * FIELDS + f : q * FIELDS + f + 1] for v in values for q in range(PIECES)],
                    1,
                )
                for f in range(FIELDS)
            ],
            *[row(place, a) for a in range(3)],
            *[row(weight_ref, a) for a in range(3)],
        )
        return carry

    lax.fori_loop(0, BLOCKS // 2, source_step, 0)
    over_peers(lambda d: slot_copy(d).wait_send())
    over_peers(lambda d: ag_copy(d).wait())

    load_res.wait()
    load_kfac.wait()
    n = FIELDS * CI
    for j in range(CJ):
        total = res_ref[:, j].reshape(n, CK)
        for r, c in ((j, 0), (j - 7, CK)):
            if 0 <= r < 8:
                more = jnp.concatenate([ag_in[2 * r, :, c : c + CK], ag_in[2 * r + 1, :, c : c + CK]], 0)
                more = jnp.where(hot == block, more, 0.0)
                total = total + acc[r * n : (r + 1) * n, c : c + CK] + more
        x[:, j * CK : (j + 1) * CK] = total
    x[:, CJ * CK :] = jnp.zeros((n, CK), F32)

    ends = mm(i_ends[...], x[...])
    for c in range(LINES):
        i_out[c] = ends[:, c * 256 : (c + 1) * 256]
    i_in[line] = i_out[line]
    end_copies = [
        to_line(d, i_out.at[(line + d) % LINES], i_in.at[line], end_send, end_recv)
        for d in range(1, LINES)
    ]
    for copy in end_copies:
        copy.start()
    x[...] = mm(i_mat[...], x[...])
    k_refs = (kfac_ref, coup_ref, k_mat, k_state, k_ends, k_pad)
    prepare_k(range(0, 3), *k_refs)
    for copy in map_copies:
        copy.wait()
    for copy in end_copies:
        copy.wait()

    def i_end(s):
        return [i_in[s, 6 * a : 6 * a + 6, :] for a in range(4)]

    i_cols = [columns_of(i_maps[s], 0, 256) for s in range(LINES)]

    def i_keep(s, up, state):
        for a in range(2):
            at = 12 * up + 6 * a
            s_out[s, at : at + 6, :] = state[a]

    chain(LINES, i_end, lambda s: i_cols[s], i_keep)
    s_in[line] = s_out[line]
    st_copies = [
        to_line(d, s_out.at[(line + d) % LINES], s_in.at[line], st_send, st_recv)
        for d in range(1, LINES)
    ]
    for copy in st_copies:
        copy.start()
    prepare_k(range(3, 6), *k_refs)
    for copy in st_copies:
        copy.wait()
    for c in range(LINES):
        part = x[:, c * 256 : (c + 1) * 256] + mm(i_state[...], s_in[c])
        for jj in range(2):
            j = 2 * c + jj
            for f in range(FIELDS):
                xk[f, j * 8 : j * 8 + 8, :] = part[f * 8 : f * 8 + 8, jj * CK : (jj + 1) * CK]

    for f in range(FIELDS):
        found = nt(k_ends[f], stack3(xk[f], 1, True)) + k_pad[f]
        for a in range(4):
            k_all[block, 6 * a + f : 6 * a + f + 1, :] = found[a : a + 1]
    k_copies = [
        pltpu.make_async_remote_copy(
            src_ref=k_all.at[block],
            dst_ref=k_all.at[block],
            send_sem=k_send.at[d],
            recv_sem=k_recv.at[d],
            device_id={"block": (block + d) % BLOCKS},
            device_id_type=MESH,
        )
        for d in range(1, BLOCKS)
    ]
    for copy in k_copies:
        copy.start()
    for f in range(FIELDS):
        xk[f] = nt(stack3(xk[f], 1, False), k_mat[f])
    for copy in k_copies:
        copy.wait()

    def k_end(s):
        return [k_all[s, 6 * a : 6 * a + 6, :] for a in range(4)]

    k_cols = [columns_of(k_all[s], 120, CK) for s in range(BLOCKS)]
    kept = [[jnp.zeros((FIELDS, CK), F32)] * 2 for _ in range(2)]

    def k_keep(s, up, state):
        kept[up] = [jnp.where(block == s, state[a], kept[up][a]) for a in range(2)]

    chain(BLOCKS, k_end, lambda s: k_cols[s], k_keep)
    k_st[...] = jnp.zeros_like(k_st)
    for f in range(FIELDS):
        for a in range(4):
            k_st[f, a : a + 1, :] = kept[a // 2][a % 2][f : f + 1]
    for f in range(FIELDS):
        done = xk[f] + mm_tn(k_st[f], k_state[f])
        out_ref[f] = done[0 : CJ * CI].reshape(CJ, CI, CK)


def sweep(
    adjoint,
    receptor_cell,
    residual,
    i_factors,
    k_factors,
    couplings,
    send_count,
    donor_cell,
    donor_weight,
):
    vmem, smem = pl.BlockSpec(memory_space=pltpu.VMEM), pl.BlockSpec(memory_space=pltpu.SMEM)
    hbm = pl.BlockSpec(memory_space=pl.ANY)
    n = FIELDS * CI
    dma = pltpu.SemaphoreType.DMA
    return pl.pallas_call(
        main_kernel,
        out_shape=jax.ShapeDtypeStruct((FIELDS, CJ, CI, CK), F32),
        in_specs=[vmem] * 2 + [hbm, vmem, hbm, smem, smem] + [vmem] * 2,
        out_specs=vmem,
        scratch_shapes=[
            pltpu.VMEM((FIELDS * 64, 512), BF),
            pltpu.VMEM((2, BLOCKS, CAP), jnp.int32),
            pltpu.VMEM((3, BLOCKS, CAP), jnp.int32),
            pltpu.VMEM((BLOCKS, 32, 256), F32),
            pltpu.VMEM((BLOCKS, 32, 256), F32),
            pltpu.VMEM((BLOCKS, 4, REST), F32),
            pltpu.VMEM((BLOCKS, 4, REST), F32),
            pltpu.VMEM((FIELDS, REST), F32),
            pltpu.VMEM((384, 256), F32),
            pltpu.VMEM((BLOCKS, PART, 256), F32),
            pltpu.VMEM((BLOCKS, PART, 256), F32),
            pltpu.VMEM((BLOCKS, PART, 256), F32),
            pltpu.VMEM((n, 16 * CK), F32),
            pltpu.VMEM((n, n), F32),
            pltpu.VMEM((n, 24), F32),
            pltpu.VMEM((24, n), F32),
            pltpu.VMEM((LINES, 24, CK), F32),
            pltpu.VMEM((LINES, 24, 256), F32),
            pltpu.VMEM((LINES, 24, 256), F32),
            pltpu.VMEM((LINES, 24, 256), F32),
            pltpu.VMEM((LINES, 24, 256), F32),
            pltpu.VMEM((FIELDS, CK, 3 * CK), BF),
            pltpu.VMEM((FIELDS, 8, CK), F32),
            pltpu.VMEM((FIELDS, 8, 3 * CK), BF),
            pltpu.VMEM((FIELDS, 8, CK), F32),
            pltpu.VMEM((BLOCKS, 24, CK), F32),
            pltpu.VMEM((FIELDS, 8, CK), F32),
            pltpu.VMEM((FIELDS, CK, CK), F32),
        ]
        + [dma((BLOCKS,))] * 8
        + [dma((LINES,))] * 6
        + [dma((BLOCKS,))] * 2
        + [
            pltpu.VMEM((FIELDS, CJ, CI, CK), F32),
            pltpu.VMEM((2, FIELDS, CK, CK), F32),
            dma((2,)),
        ],
        compiler_params=pltpu.CompilerParams(
            vmem_limit_bytes=56 * 2**20, collective_id=0, has_side_effects=True
        ),
        name="sweep",
    )(
        adjoint,
        receptor_cell,
        residual,
        i_factors,
        k_factors,
        couplings,
        send_count,
        donor_cell,
        donor_weight,
    )


def per_device(
    residual,
    adjoint,
    i_factors,
    k_factors,
    couplings,
    receptor_cell,
    send_count,
    donor_cell,
    donor_weight,
):
    update = sweep(
        adjoint.transpose(0, 2, 1, 3),
        receptor_cell[0, 0],
        residual.transpose(0, 2, 1, 3),
        i_factors[0],
        k_factors[0],
        couplings[0, 0].transpose(1, 0, 2),
        send_count[0, 0],
        donor_cell[0, 0],
        donor_weight[0, 0],
    )
    return update.transpose(0, 2, 1, 3)


def solution(mesh):
    return jax.shard_map(
        per_device,
        mesh=mesh,
        in_specs=(
            P(None, "line", None, "block"),
            P(None, "line", None, "block"),
            P("block", None, None, "line", None),
            P("line", None, None, "block", None),
            P("line", "block", None, None, None),
            P("line", "block", None, None),
            P("line", "block", None),
            P("line", "block", None, None),
            P("line", "block", None, None, None),
        ),
        out_specs=P(None, "line", None, "block"),
        check_vma=False,
    )
```

```python
import functools

import jax
import jax.numpy as jnp
from jax import lax
from jax.experimental import pallas as pl
from jax.experimental.pallas import tpu as pltpu
from jax.sharding import PartitionSpec as P

F32, BF = jnp.float32, jnp.bfloat16
FIELDS, CI, CJ, CK, CAP = 6, 8, 15, 128, 2048
HEAD = 5 * CAP // 8
REST = CAP - HEAD
PART = 384 // 16
DIRECT = 2
TABLED = FIELDS - DIRECT
TOGETHER = 4
PIECES = HEAD // 256
EARLY = 1
REST_AT = 0
GRID_AT = 2
LINES, BLOCKS = 8, 16
HIGHEST = lax.Precision.HIGHEST
MESH = pl.DeviceIdType.MESH


def iota(shape, axis):
    return lax.broadcasted_iota(jnp.int32, shape, axis)


def split(x):
    high = x.astype(BF)
    return high, (x - high.astype(F32)).astype(BF)


def as_bf(x):
    return x.astype(F32).astype(BF)


def mm(a, b):
    return jnp.dot(a, b, precision=HIGHEST, preferred_element_type=F32)


def mm_nt(a, b):
    return lax.dot_general(
        a, b, (((1,), (1,)), ((), ())), precision=HIGHEST, preferred_element_type=F32
    )


def mm_tn(a, b):
    return lax.dot_general(
        a, b, (((0,), (0,)), ((), ())), precision=HIGHEST, preferred_element_type=F32
    )


def cell_parts(cell):
    ij = cell >> 7
    i = (ij * 137) >> 11
    return i, ij - i * CJ, cell & 127


def gather_table(adj_ref, table):
    for f in range(TABLED):
        planes = [adj_ref[f, j] for j in range(CJ)] + [jnp.zeros((CI, CK), F32)]
        for half in range(2):
            high, low = split(jnp.concatenate(planes[8 * half : 8 * half + 8], 0))
            row, col = f * 64, half * CK
            table[row : row + 64, col : col + CK] = high
            table[row : row + 64, 256 + col : 256 + col + CK] = low


def gather_slots(adj_ref, table, group_row, slot_row):
    C = group_row.shape[1]
    slot = as_bf(jnp.broadcast_to(slot_row, (16, C)))
    one, zero = jnp.ones((16, C), BF), jnp.zeros((16, C), BF)
    base = iota((16, C), 0)
    hot = [jnp.where(as_bf(base + 16 * n) == slot, one, zero) for n in range(16)]
    hot = jnp.concatenate(hot, 0)
    found = jnp.dot(
        table[...], jnp.concatenate([hot, hot], 0), preferred_element_type=F32
    ).reshape(TABLED, 64, C)
    mine = iota((64, C), 0) == jnp.broadcast_to(group_row, (64, C))
    rows = [
        jnp.sum(jnp.where(mine, found[f], 0.0), axis=0, keepdims=True) for f in range(TABLED)
    ]
    if DIRECT:
        plane_row = group_row + ((slot_row >> 7) << 6)
        lane_row = slot_row & (CK - 1)
        base = iota((CI, CK), 0)
        pieces = [[] for _ in range(DIRECT)]
        for c in range(0, C, CK):
            plane = jnp.broadcast_to(plane_row[:, c : c + CK], (CI, CK))
            lane = jnp.broadcast_to(lane_row[:, c : c + CK], (CI, CK))
            total = [jnp.zeros((CI, CK), F32)] * DIRECT
            for j in range(CJ):
                here = base + CI * j == plane
                for q in range(DIRECT):
                    moved = jnp.take_along_axis(adj_ref[TABLED + q, j], lane, axis=1)
                    total[q] = jnp.where(here, moved, total[q])
            for q in range(DIRECT):
                pieces[q].append(jnp.sum(total[q], axis=0, keepdims=True))
        rows += [jnp.concatenate(p, 1) for p in pieces]
    return rows


def scatter_slots(values, base_i, base_j, base_t, x, y, z):
    C = x.shape[1]

    def wide(row, n):
        return jnp.broadcast_to(row, (n, C))

    at = iota((8, C), 0)

    def hat(base, t):
        base, t = wide(base, 8), wide(t, 8)
        return jnp.where(at == base, 1.0 - t, jnp.where(at == base + 1, t, 0.0))

    wi, wj = hat(base_i, x), hat(base_j, y)
    u = jnp.concatenate([wide(v, 8) * wi for v in values], 0)
    high, low = [], []
    for r in range(8):
        h, l = split(u * wide(wj[r : r + 1], 48))
        high.append(h)
        low.append(l)
    high, low = jnp.concatenate(high, 0), jnp.concatenate(low, 0)
    z = wide(z, 16)
    z1h, z1l = split(z)
    z0h, z0l = split(1.0 - z)
    t = wide(base_t, 16)
    t0, t1 = as_bf(t), as_bf(t + 1)
    zero = jnp.zeros((16, C), BF)
    base = iota((16, C), 0)
    col_h, col_l = [], []
    for n in range(16):
        r = as_bf(base + 16 * n)
        first, second = r == t0, r == t1
        col_h.append(jnp.where(first, z0h, jnp.where(second, z1h, zero)))
        col_l.append(jnp.where(first, z0l, jnp.where(second, z1l, zero)))
    col_h, col_l = jnp.concatenate(col_h, 0), jnp.concatenate(col_l, 0)
    return lax.dot_general(
        jnp.concatenate([high, high, low], 1),
        jnp.concatenate([col_h, col_l, col_h], 1),
        (((1,), (1,)), ((), ())),
        preferred_element_type=F32,
    )


def donor_parts(cell):
    i, j, k = cell_parts(cell)
    upper = jnp.where(j >= 7, 1, 0)
    return i, j - 7 * upper, upper * CK + k


def entries(shape, items):
    rows, cols = iota(shape, 0), iota(shape, 1)
    out = jnp.zeros(shape, F32)
    for r, c, value in items:
        out = jnp.where((rows == r) & (cols == c), value, out)
    return out


def prepare_i(ifac_ref, coup_ref, i_mat, i_state, i_ends, i_maps_own):
    n = FIELDS * CI
    r, c = iota((n, n), 0), iota((n, n), 1)
    same = (r >> 3) == (c >> 3)
    flip = jnp.where(same & ((r & 7) + (c & 7) == 7), 1.0, 0.0)
    spread = jnp.where(iota((CI, n), 0) == (iota((CI, n), 1) & 7), 1.0, 0.0)

    def diagonal(direction):
        flat = ifac_ref[direction].reshape(n, CI)
        return jnp.where(same, mm(flat, spread), 0.0)

    low = diagonal(0)
    up = mm(flip, mm(diagonal(1), flip))
    whole = mm(up, low)
    shape = (n, 24)
    e_low = entries(
        shape,
        [(8 * f, f, coup_ref[0, 0, f]) for f in range(FIELDS)]
        + [(8 * f, 6 + f, coup_ref[1, 0, f]) for f in range(FIELDS)]
        + [(8 * f + 1, f, coup_ref[2, 0, f]) for f in range(FIELDS)],
    )
    e_up = entries(
        shape,
        [(8 * f + 7, 12 + f, coup_ref[0, 1, f]) for f in range(FIELDS)]
        + [(8 * f + 7, 18 + f, coup_ref[1, 1, f]) for f in range(FIELDS)]
        + [(8 * f + 6, 12 + f, coup_ref[2, 1, f]) for f in range(FIELDS)],
    )
    infl_low = mm(low, e_low)
    state = -mm(up, infl_low + e_up)
    sel_shape = (24, n)
    comp = [(a, f) for a in range(2) for f in range(FIELDS)]
    sel_e = entries(sel_shape, [(a * 6 + f, 8 * f + 7 - a, 1.0) for a, f in comp])
    sel_p = entries(sel_shape, [(12 + a * 6 + f, 8 * f + a, 1.0) for a, f in comp])
    i_mat[...] = whole
    i_state[...] = state
    i_ends[...] = mm(sel_e, low) + mm(sel_p, whole)
    between = mm(sel_p, state) - mm(sel_e, infl_low)
    fold_r, fold_c = iota((24, CK), 0), iota((24, CK), 1)
    fold = jnp.where((fold_r >= 6 * fold_c) & (fold_r < 6 * fold_c + 6), 1.0, 0.0)
    i_maps_own[...] = mm(between, fold)


def stack3(x, axis, middle_low):
    high, low = split(x)
    return jnp.concatenate([high, low, high] if middle_low else [high, high, low], axis)


def mm3(a, b):
    return jnp.dot(stack3(a, 1, False), stack3(b, 0, True), preferred_element_type=F32)


def nt(a, b):
    return lax.dot_general(a, b, (((1,), (1,)), ((), ())), preferred_element_type=F32)


def mm3_nt(a, b):
    return nt(stack3(a, 1, False), stack3(b, 1, True))


def prepare_k(fields, kfac_ref, coup_ref, k_mat, k_state, k_ends, k_pad):
    n = CK
    flip = jnp.where(iota((n, n), 0) + iota((n, n), 1) == n - 1, 1.0, 0.0).astype(BF)
    flip_cols = jnp.concatenate([flip, flip], 0)
    flip_rows = jnp.concatenate([flip, flip], 1)
    sel_e = entries((8, n), [(0, n - 1, 1.0), (1, n - 2, 1.0)])
    sel_p = entries((8, n), [(2, 0, 1.0), (3, 1, 1.0)])
    pad = jnp.zeros((n - 8, n), F32)
    for f in fields:
        low = kfac_ref[0, f]
        up = jnp.dot(
            jnp.concatenate(split(kfac_ref[1, f]), 1), flip_cols, preferred_element_type=F32
        )
        up = jnp.dot(flip_rows, jnp.concatenate(split(up), 0), preferred_element_type=F32)
        whole = mm3(up, low)
        e_low = entries(
            (8, n),
            [(0, 0, coup_ref[0, 2, f]), (0, 1, coup_ref[2, 2, f]), (1, 0, coup_ref[1, 2, f])],
        )
        e_up = entries(
            (8, n),
            [
                (2, n - 1, coup_ref[0, 3, f]),
                (2, n - 2, coup_ref[2, 3, f]),
                (3, n - 1, coup_ref[1, 3, f]),
            ],
        )
        infl_low = mm3_nt(e_low, low)
        state = -mm3_nt(infl_low + e_up, up)
        k_mat[f] = stack3(whole, 1, True)
        k_state[f] = state
        k_ends[f] = stack3(
            jnp.concatenate([low[n - 1 : n], low[n - 2 : n - 1], whole[0:2], pad[0:4]], 0), 1, False
        )
        k_pad[f] = mm3_nt(sel_p, jnp.concatenate([pad, state], 0)) - mm3_nt(
            sel_e, jnp.concatenate([pad, infl_low], 0)
        )


def chain(count, ends, maps, keep):
    shape = ends(0)[0].shape
    s = [jnp.zeros(shape, F32)] * 2
    tops = []
    for n in range(count):
        e0, e1, p0, p1 = ends(n)
        m = maps(n)
        keep(n, 0, s)
        tops.append(
            [p0 + m[2][0] * s[0] + m[2][1] * s[1], p1 + m[3][0] * s[0] + m[3][1] * s[1]]
        )
        if n < count - 1:
            s = [e0 + m[0][0] * s[0] + m[0][1] * s[1], e1 + m[1][0] * s[0] + m[1][1] * s[1]]
    t = [jnp.zeros(shape, F32)] * 2
    for n in range(count - 1, -1, -1):
        m = maps(n)
        keep(n, 1, t)
        if n > 0:
            q0, q1 = tops[n]
            t = [q0 + m[2][2] * t[0] + m[2][3] * t[1], q1 + m[3][2] * t[0] + m[3][3] * t[1]]


def columns_of(block, first, width):
    def one(a, b):
        return jnp.broadcast_to(
            block[6 * a : 6 * a + 6, first + b : first + b + 1], (FIELDS, width)
        )

    return [
        [one(a, b) if a >= 2 or b < 2 else None for b in range(4)] for a in range(4)
    ]


def main_kernel(
    adj_ref,
    rec_ref,
    res_hbm,
    ifac_ref,
    kfac_hbm,
    coup_ref,
    count_ref,
    cell_ref,
    weight_ref,
    z_hbm,
    k_st,
    k_state,
    table,
    where_ref,
    place,
    outgoing,
    incoming,
    info_out,
    info_in,
    rest,
    acc,
    acc_rest,
    rs_in,
    ag_in,
    x,
    i_mat,
    i_state,
    i_ends,
    i_maps,
    i_out,
    i_in,
    s_out,
    s_in,
    k_mat,
    k_ends,
    k_pad,
    k_all,
    xk,
    info_send,
    info_recv,
    a2a_send,
    a2a_recv,
    rs_send,
    rs_recv,
    ag_send,
    ag_recv,
    map_send,
    map_recv,
    end_send,
    end_recv,
    st_send,
    st_recv,
    k_send,
    k_recv,
    res_ref,
    kfac_ref,
    load_sem,
):
    load_res = pltpu.make_async_copy(res_hbm, res_ref, load_sem.at[0])
    load_kfac = pltpu.make_async_copy(kfac_hbm, kfac_ref, load_sem.at[1])
    load_res.start()
    load_kfac.start()
    line, block = lax.axis_index("line"), lax.axis_index("block")
    barrier = pltpu.get_barrier_semaphore()
    for d in range(1, LINES):
        pl.semaphore_signal(
            barrier, inc=1, device_id={"line": lax.rem(line + d, LINES)}, device_id_type=MESH
        )
    for d in range(1, BLOCKS):
        pl.semaphore_signal(
            barrier, inc=1, device_id={"block": lax.rem(block + d, BLOCKS)}, device_id_type=MESH
        )

    def to_line(d, src, dst, send, recv):
        return pltpu.make_async_remote_copy(
            src_ref=src,
            dst_ref=dst,
            send_sem=send.at[d],
            recv_sem=recv.at[d],
            device_id={"line": lax.rem(line + d, LINES)},
            device_id_type=MESH,
        )

    def to_block(d, src, dst, send, recv):
        return pltpu.make_async_remote_copy(
            src_ref=src,
            dst_ref=dst,
            send_sem=send.at[d],
            recv_sem=recv.at[d],
            device_id={"block": lax.rem(block + d, BLOCKS)},
            device_id_type=MESH,
        )

    def peer(d):
        return lax.rem(block + d, BLOCKS)

    def info_copy(d):
        return to_block(d, info_out.at[peer(d)], info_in.at[block], info_send, info_recv)

    def slot_copy(d):
        return to_block(d, outgoing.at[peer(d)], incoming.at[block], a2a_send, a2a_recv)

    def rs_copy(d):
        return to_block(d, acc_rest.at[peer(d)], rs_in.at[block], rs_send, rs_recv)

    def ag_copy(d):
        return to_block(d, ag_in.at[block], ag_in.at[block], ag_send, ag_recv)

    def over_peers(action):
        def step(d, carry):
            action(d)
            return carry

        lax.fori_loop(1, BLOCKS, step, 0)

    hot = jnp.int32(0)
    for o in range(BLOCKS):
        hot = jnp.where(count_ref[o] == CAP, o, hot)

    for p in range(BLOCKS):
        info_out[p, 0:1, :] = cell_ref[p : p + 1, HEAD:].astype(F32)
        for a in range(3):
            info_out[p, a + 1 : a + 2, :] = weight_ref[a, p : p + 1, HEAD:]
    gather_table(adj_ref, table)
    i, j, k = cell_parts(rec_ref[...])
    where_ref[0] = (j & 7) * CI + i
    where_ref[1] = (j >> 3) * CK + k
    for a, part in enumerate(donor_parts(cell_ref[...])):
        place[a] = part
    prepare_i(ifac_ref, coup_ref, i_mat, i_state, i_ends, i_maps.at[line])
    outgoing[:, FIELDS * PIECES :, :] = jnp.zeros((BLOCKS, 32 - FIELDS * PIECES, 256), F32)

    def owner_step(t, carry):
        owners = [peer(2 * t), peer(2 * t + 1)]
        group_row, slot_row = [
            jnp.concatenate([where_ref[a, pl.ds(o, 1), 0:HEAD] for o in owners], 1)
            for a in range(2)
        ]
        rows = gather_slots(adj_ref, table, group_row, slot_row)
        for n, o in enumerate(owners):
            live = iota((1, HEAD), 1) < count_ref[o]
            for f in range(FIELDS):
                row = jnp.where(live, rows[f][:, n * HEAD : (n + 1) * HEAD], 0.0)
                for q in range(PIECES):
                    at = q * FIELDS + f
                    outgoing[o, at : at + 1, :] = row[:, q * 256 : (q + 1) * 256]
        return carry

    lax.fori_loop(0, EARLY, owner_step, 0)
    incoming[block] = outgoing[block]
    for f, row in enumerate(
        gather_slots(adj_ref, table, where_ref[0, pl.ds(hot, 1), HEAD:], where_ref[1, pl.ds(hot, 1), HEAD:])
    ):
        rest[f : f + 1, :] = row

    pl.semaphore_wait(barrier, LINES + BLOCKS - 2)
    over_peers(lambda d: info_copy(d).start())

    def early_step(d, carry):
        slot_copy(d).start()
        return carry

    lax.fori_loop(1, 2 * EARLY, early_step, 0)
    map_copies = [
        to_line(d, i_maps.at[line], i_maps.at[line], map_send, map_recv) for d in range(1, LINES)
    ]
    for copy in map_copies:
        copy.start()
    info_in[block] = info_out[block]

    def late_step(d, carry):
        owner_step(d, carry)
        slot_copy(2 * d).start()
        slot_copy(2 * d + 1).start()
        return carry

    lax.fori_loop(EARLY, BLOCKS // 2, late_step, 0)

    acc[...] = jnp.zeros_like(acc)

    def source_step(t, carry):
        sources = [lax.rem(block + BLOCKS - TOGETHER * t - n, BLOCKS) for n in range(TOGETHER)]

        @pl.when(t > 0)
        def _():
            slot_copy(TOGETHER * t).wait_recv()

        for n in range(1, TOGETHER):
            slot_copy(TOGETHER * t + n).wait_recv()

        @pl.when(t == REST_AT)
        def _():
            over_peers(lambda d: info_copy(d).wait())
            info = info_in[hot]
            found = scatter_slots(
                [rest[f : f + 1, :] for f in range(FIELDS)],
                *donor_parts(info[0:1].astype(jnp.int32)),
                info[1:2],
                info[2:3],
                info[3:4],
            )
            for p in range(BLOCKS):
                acc_rest[p] = found[p * PART : (p + 1) * PART]
            rs_in[block] = acc_rest[block]
            over_peers(lambda d: rs_copy(d).start())

        @pl.when(t == GRID_AT)
        def _():
            over_peers(lambda e: rs_copy(e).wait())
            total = rs_in[0]
            for p in range(1, BLOCKS):
                total = total + rs_in[p]
            ag_in[block] = total
            over_peers(lambda e: ag_copy(e).start())

        def row(ref, a):
            return jnp.concatenate([ref[a, pl.ds(s, 1), 0:HEAD] for s in sources], 1)

        values = [incoming[s] for s in sources]
        acc[...] += scatter_slots(
            [
                jnp.concatenate(
                    [v[q * FIELDS + f : q * FIELDS + f + 1] for v in values for q in range(PIECES)],
                    1,
                )
                for f in range(FIELDS)
            ],
            *[row(place, a) for a in range(3)],
            *[row(weight_ref, a) for a in range(3)],
        )
        return carry

    lax.fori_loop(0, BLOCKS // TOGETHER, source_step, 0)
    over_peers(lambda d: slot_copy(d).wait_send())
    over_peers(lambda d: ag_copy(d).wait())

    load_res.wait()
    load_kfac.wait()
    n = FIELDS * CI
    for j in range(CJ):
        total = res_ref[:, j].reshape(n, CK)
        for r, c in ((j, 0), (j - 7, CK)):
            if 0 <= r < 8:
                more = jnp.concatenate([ag_in[2 * r, :, c : c + CK], ag_in[2 * r + 1, :, c : c + CK]], 0)
                more = jnp.where(hot == block, more, 0.0)
                total = total + acc[r * n : (r + 1) * n, c : c + CK] + more
        x[:, j * CK : (j + 1) * CK] = total
    x[:, CJ * CK :] = jnp.zeros((n, CK), F32)

    ends = mm(i_ends[...], x[...])
    for c in range(LINES):
        i_out[c] = ends[:, c * 256 : (c + 1) * 256]
    i_in[line] = i_out[line]
    end_copies = [
        to_line(d, i_out.at[(line + d) % LINES], i_in.at[line], end_send, end_recv)
        for d in range(1, LINES)
    ]
    for copy in end_copies:
        copy.start()
    x[...] = mm(i_mat[...], x[...])
    k_refs = (kfac_ref, coup_ref, k_mat, k_state, k_ends, k_pad)
    prepare_k(range(0, 3), *k_refs)
    for copy in map_copies:
        copy.wait()
    for copy in end_copies:
        copy.wait()

    def i_end(s):
        return [i_in[s, 6 * a : 6 * a + 6, :] for a in range(4)]

    i_cols = [columns_of(i_maps[s], 0, 256) for s in range(LINES)]

    def i_keep(s, up, state):
        for a in range(2):
            at = 12 * up + 6 * a
            s_out[s, at : at + 6, :] = state[a]

    chain(LINES, i_end, lambda s: i_cols[s], i_keep)
    s_in[line] = s_out[line]
    st_copies = [
        to_line(d, s_out.at[(line + d) % LINES], s_in.at[line], st_send, st_recv)
        for d in range(1, LINES)
    ]
    for copy in st_copies:
        copy.start()
    prepare_k(range(3, 6), *k_refs)
    for copy in st_copies:
        copy.wait()
    for c in range(LINES):
        part = x[:, c * 256 : (c + 1) * 256] + mm(i_state[...], s_in[c])
        for jj in range(2):
            j = 2 * c + jj
            for f in range(FIELDS):
                xk[f, j * 8 : j * 8 + 8, :] = part[f * 8 : f * 8 + 8, jj * CK : (jj + 1) * CK]

    for f in range(FIELDS):
        found = nt(k_ends[f], stack3(xk[f], 1, True)) + k_pad[f]
        for a in range(4):
            k_all[block, 6 * a + f : 6 * a + f + 1, :] = found[a : a + 1]
    k_copies = [
        pltpu.make_async_remote_copy(
            src_ref=k_all.at[block],
            dst_ref=k_all.at[block],
            send_sem=k_send.at[d],
            recv_sem=k_recv.at[d],
            device_id={"block": (block + d) % BLOCKS},
            device_id_type=MESH,
        )
        for d in range(1, BLOCKS)
    ]
    for copy in k_copies:
        copy.start()
    for f in range(FIELDS):
        xk[f] = nt(stack3(xk[f], 1, False), k_mat[f])
    store_z = pltpu.make_async_copy(xk, z_hbm, load_sem.at[2])
    store_z.start()
    for copy in k_copies:
        copy.wait()

    def k_end(s):
        return [k_all[s, 6 * a : 6 * a + 6, :] for a in range(4)]

    k_cols = [columns_of(k_all[s], 120, CK) for s in range(BLOCKS)]
    kept = [[jnp.zeros((FIELDS, CK), F32)] * 2 for _ in range(2)]

    def k_keep(s, up, state):
        kept[up] = [jnp.where(block == s, state[a], kept[up][a]) for a in range(2)]

    chain(BLOCKS, k_end, lambda s: k_cols[s], k_keep)
    k_st[...] = jnp.zeros_like(k_st)
    for f in range(FIELDS):
        for a in range(4):
            k_st[f, a : a + 1, :] = kept[a // 2][a % 2][f : f + 1]
    store_z.wait()


def finish_kernel(z_ref, st_ref, state_ref, out_ref):
    for f in range(FIELDS):
        done = z_ref[f] + mm_tn(st_ref[f], state_ref[f])
        out_ref[f] = done[0 : CJ * CI].reshape(CJ, CI, CK)


def finish(z, states, state_map):
    vmem = pl.BlockSpec(memory_space=pltpu.VMEM)
    return pl.pallas_call(
        finish_kernel,
        out_shape=jax.ShapeDtypeStruct((FIELDS, CJ, CI, CK), F32),
        in_specs=[vmem] * 3,
        out_specs=vmem,
        name="finish",
    )(z, states, state_map)


def sweep(
    adjoint,
    receptor_cell,
    residual,
    i_factors,
    k_factors,
    couplings,
    send_count,
    donor_cell,
    donor_weight,
):
    vmem, smem = pl.BlockSpec(memory_space=pltpu.VMEM), pl.BlockSpec(memory_space=pltpu.SMEM)
    hbm = pl.BlockSpec(memory_space=pl.ANY)
    n = FIELDS * CI
    dma = pltpu.SemaphoreType.DMA
    return pl.pallas_call(
        main_kernel,
        out_shape=[
            jax.ShapeDtypeStruct((FIELDS, CK, CK), F32),
            jax.ShapeDtypeStruct((FIELDS, 8, CK), F32),
            jax.ShapeDtypeStruct((FIELDS, 8, CK), F32),
        ],
        in_specs=[vmem] * 2 + [hbm, vmem, hbm, smem, smem] + [vmem] * 2,
        out_specs=[hbm, vmem, vmem],
        scratch_shapes=[
            pltpu.VMEM((TABLED * 64, 512), BF),
            pltpu.VMEM((2, BLOCKS, CAP), jnp.int32),
            pltpu.VMEM((3, BLOCKS, CAP), jnp.int32),
            pltpu.VMEM((BLOCKS, 32, 256), F32),
            pltpu.VMEM((BLOCKS, 32, 256), F32),
            pltpu.VMEM((BLOCKS, 4, REST), F32),
            pltpu.VMEM((BLOCKS, 4, REST), F32),
            pltpu.VMEM((FIELDS, REST), F32),
            pltpu.VMEM((384, 256), F32),
            pltpu.VMEM((BLOCKS, PART, 256), F32),
            pltpu.VMEM((BLOCKS, PART, 256), F32),
            pltpu.VMEM((BLOCKS, PART, 256), F32),
            pltpu.VMEM((n, 16 * CK), F32),
            pltpu.VMEM((n, n), F32),
            pltpu.VMEM((n, 24), F32),
            pltpu.VMEM((24, n), F32),
            pltpu.VMEM((LINES, 24, CK), F32),
            pltpu.VMEM((LINES, 24, 256), F32),
            pltpu.VMEM((LINES, 24, 256), F32),
            pltpu.VMEM((LINES, 24, 256), F32),
            pltpu.VMEM((LINES, 24, 256), F32),
            pltpu.VMEM((FIELDS, CK, 3 * CK), BF),
            pltpu.VMEM((FIELDS, 8, 3 * CK), BF),
            pltpu.VMEM((FIELDS, 8, CK), F32),
            pltpu.VMEM((BLOCKS, 24, CK), F32),
            pltpu.VMEM((FIELDS, CK, CK), F32),
        ]
        + [dma((BLOCKS,))] * 8
        + [dma((LINES,))] * 6
        + [dma((BLOCKS,))] * 2
        + [
            pltpu.VMEM((FIELDS, CJ, CI, CK), F32),
            pltpu.VMEM((2, FIELDS, CK, CK), F32),
            dma((3,)),
        ],
        compiler_params=pltpu.CompilerParams(
            vmem_limit_bytes=56 * 2**20, collective_id=0, has_side_effects=True
        ),
        name="sweep",
    )(
        adjoint,
        receptor_cell,
        residual,
        i_factors,
        k_factors,
        couplings,
        send_count,
        donor_cell,
        donor_weight,
    )


def per_device(
    residual,
    adjoint,
    i_factors,
    k_factors,
    couplings,
    receptor_cell,
    send_count,
    donor_cell,
    donor_weight,
):
    update = finish(*sweep(
        adjoint.transpose(0, 2, 1, 3),
        receptor_cell[0, 0],
        residual.transpose(0, 2, 1, 3),
        i_factors[0],
        k_factors[0],
        couplings[0, 0].transpose(1, 0, 2),
        send_count[0, 0],
        donor_cell[0, 0],
        donor_weight[0, 0],
    ))
    return update.transpose(0, 2, 1, 3)


def solution(mesh):
    return jax.shard_map(
        per_device,
        mesh=mesh,
        in_specs=(
            P(None, "line", None, "block"),
            P(None, "line", None, "block"),
            P("block", None, None, "line", None),
            P("line", None, None, "block", None),
            P("line", "block", None, None, None),
            P("line", "block", None, None),
            P("line", "block", None),
            P("line", "block", None, None),
            P("line", "block", None, None, None),
        ),
        out_specs=P(None, "line", None, "block"),
        check_vma=False,
    )
```

```python
import functools

import jax
import jax.numpy as jnp
from jax import lax
from jax.experimental import pallas as pl
from jax.experimental.pallas import tpu as pltpu
from jax.sharding import PartitionSpec as P

F32, BF = jnp.float32, jnp.bfloat16
FIELDS, CI, CJ, CK, CAP = 6, 8, 15, 128, 2048
HEAD = 5 * CAP // 8
REST = CAP - HEAD
PART = 384 // 16
DIRECT = 2
TABLED = FIELDS - DIRECT
TOGETHER = 4
PIECES = HEAD // 256
EARLY = 1
REST_AT = 0
GRID_AT = 2
LINES, BLOCKS = 8, 16
HIGHEST = lax.Precision.HIGHEST
MESH = pl.DeviceIdType.MESH


def iota(shape, axis):
    return lax.broadcasted_iota(jnp.int32, shape, axis)


def split(x):
    high = x.astype(BF)
    return high, (x - high.astype(F32)).astype(BF)


def as_bf(x):
    return x.astype(F32).astype(BF)


def mm(a, b):
    return jnp.dot(a, b, precision=HIGHEST, preferred_element_type=F32)


def mm_nt(a, b):
    return lax.dot_general(
        a, b, (((1,), (1,)), ((), ())), precision=HIGHEST, preferred_element_type=F32
    )


def mm_tn(a, b):
    return lax.dot_general(
        a, b, (((0,), (0,)), ((), ())), precision=HIGHEST, preferred_element_type=F32
    )


def cell_parts(cell):
    ij = cell >> 7
    i = (ij * 137) >> 11
    return i, ij - i * CJ, cell & 127


def gather_table(adj_ref, table):
    for f in range(TABLED):
        planes = [adj_ref[f, j] for j in range(CJ)] + [jnp.zeros((CI, CK), F32)]
        for half in range(2):
            high, low = split(jnp.concatenate(planes[8 * half : 8 * half + 8], 0))
            row, col = f * 64, half * CK
            table[row : row + 64, col : col + CK] = high
            table[row : row + 64, 256 + col : 256 + col + CK] = low


def gather_slots(adj_ref, table, group_row, slot_row):
    C = group_row.shape[1]
    slot = as_bf(jnp.broadcast_to(slot_row, (16, C)))
    one, zero = jnp.ones((16, C), BF), jnp.zeros((16, C), BF)
    base = iota((16, C), 0)
    hot = [jnp.where(as_bf(base + 16 * n) == slot, one, zero) for n in range(16)]
    hot = jnp.concatenate(hot, 0)
    found = jnp.dot(
        table[...], jnp.concatenate([hot, hot], 0), preferred_element_type=F32
    ).reshape(TABLED, 64, C)
    mine = iota((64, C), 0) == jnp.broadcast_to(group_row, (64, C))
    rows = [
        jnp.sum(jnp.where(mine, found[f], 0.0), axis=0, keepdims=True) for f in range(TABLED)
    ]
    if DIRECT:
        plane_row = group_row + ((slot_row >> 7) << 6)
        lane_row = slot_row & (CK - 1)
        base = iota((CI, CK), 0)
        pieces = [[] for _ in range(DIRECT)]
        for c in range(0, C, CK):
            plane = jnp.broadcast_to(plane_row[:, c : c + CK], (CI, CK))
            lane = jnp.broadcast_to(lane_row[:, c : c + CK], (CI, CK))
            total = [jnp.zeros((CI, CK), F32)] * DIRECT
            for j in range(CJ):
                here = base + CI * j == plane
                for q in range(DIRECT):
                    moved = jnp.take_along_axis(adj_ref[TABLED + q, j], lane, axis=1)
                    total[q] = jnp.where(here, moved, total[q])
            for q in range(DIRECT):
                pieces[q].append(jnp.sum(total[q], axis=0, keepdims=True))
        rows += [jnp.concatenate(p, 1) for p in pieces]
    return rows


def scatter_slots(values, base_i, base_j, base_t, x, y, z):
    C = x.shape[1]

    def wide(row, n):
        return jnp.broadcast_to(row, (n, C))

    at = iota((8, C), 0)

    def hat(base, t):
        base, t = wide(base, 8), wide(t, 8)
        return jnp.where(at == base, 1.0 - t, jnp.where(at == base + 1, t, 0.0))

    wi, wj = hat(base_i, x), hat(base_j, y)
    u = jnp.concatenate([wide(v, 8) * wi for v in values], 0)
    high, low = [], []
    for r in range(8):
        h, l = split(u * wide(wj[r : r + 1], 48))
        high.append(h)
        low.append(l)
    high, low = jnp.concatenate(high, 0), jnp.concatenate(low, 0)
    z = wide(z, 16)
    z1h, z1l = split(z)
    z0h, z0l = split(1.0 - z)
    t = wide(base_t, 16)
    t0, t1 = as_bf(t), as_bf(t + 1)
    zero = jnp.zeros((16, C), BF)
    base = iota((16, C), 0)
    col_h, col_l = [], []
    for n in range(16):
        r = as_bf(base + 16 * n)
        first, second = r == t0, r == t1
        col_h.append(jnp.where(first, z0h, jnp.where(second, z1h, zero)))
        col_l.append(jnp.where(first, z0l, jnp.where(second, z1l, zero)))
    col_h, col_l = jnp.concatenate(col_h, 0), jnp.concatenate(col_l, 0)
    return lax.dot_general(
        jnp.concatenate([high, high, low], 1),
        jnp.concatenate([col_h, col_l, col_h], 1),
        (((1,), (1,)), ((), ())),
        preferred_element_type=F32,
    )


def donor_parts(cell):
    i, j, k = cell_parts(cell)
    upper = jnp.where(j >= 7, 1, 0)
    return i, j - 7 * upper, upper * CK + k


def entries(shape, items):
    rows, cols = iota(shape, 0), iota(shape, 1)
    out = jnp.zeros(shape, F32)
    for r, c, value in items:
        out = jnp.where((rows == r) & (cols == c), value, out)
    return out


def prepare_i(ifac_ref, coup_ref, i_mat, i_state, i_ends, i_maps_own):
    n = FIELDS * CI
    r, c = iota((n, n), 0), iota((n, n), 1)
    same = (r >> 3) == (c >> 3)
    flip = jnp.where(same & ((r & 7) + (c & 7) == 7), 1.0, 0.0)
    spread = jnp.where(iota((CI, n), 0) == (iota((CI, n), 1) & 7), 1.0, 0.0)

    def diagonal(direction):
        flat = ifac_ref[direction].reshape(n, CI)
        return jnp.where(same, mm(flat, spread), 0.0)

    low = diagonal(0)
    up = mm(flip, mm(diagonal(1), flip))
    whole = mm(up, low)
    shape = (n, 24)
    e_low = entries(
        shape,
        [(8 * f, f, coup_ref[0, 0, f]) for f in range(FIELDS)]
        + [(8 * f, 6 + f, coup_ref[1, 0, f]) for f in range(FIELDS)]
        + [(8 * f + 1, f, coup_ref[2, 0, f]) for f in range(FIELDS)],
    )
    e_up = entries(
        shape,
        [(8 * f + 7, 12 + f, coup_ref[0, 1, f]) for f in range(FIELDS)]
        + [(8 * f + 7, 18 + f, coup_ref[1, 1, f]) for f in range(FIELDS)]
        + [(8 * f + 6, 12 + f, coup_ref[2, 1, f]) for f in range(FIELDS)],
    )
    infl_low = mm(low, e_low)
    state = -mm(up, infl_low + e_up)
    sel_shape = (24, n)
    comp = [(a, f) for a in range(2) for f in range(FIELDS)]
    sel_e = entries(sel_shape, [(a * 6 + f, 8 * f + 7 - a, 1.0) for a, f in comp])
    sel_p = entries(sel_shape, [(12 + a * 6 + f, 8 * f + a, 1.0) for a, f in comp])
    i_mat[...] = whole
    i_state[...] = state
    i_ends[...] = mm(sel_e, low) + mm(sel_p, whole)
    between = mm(sel_p, state) - mm(sel_e, infl_low)
    fold_r, fold_c = iota((24, CK), 0), iota((24, CK), 1)
    fold = jnp.where((fold_r >= 6 * fold_c) & (fold_r < 6 * fold_c + 6), 1.0, 0.0)
    i_maps_own[...] = mm(between, fold)


def stack3(x, axis, middle_low):
    high, low = split(x)
    return jnp.concatenate([high, low, high] if middle_low else [high, high, low], axis)


def mm3(a, b):
    return jnp.dot(stack3(a, 1, False), stack3(b, 0, True), preferred_element_type=F32)


def nt(a, b):
    return lax.dot_general(a, b, (((1,), (1,)), ((), ())), preferred_element_type=F32)


def mm_fast(a, b):
    a_high, a_low = split(a)
    b_high, b_low = split(b)

    def one(p, q):
        return jnp.dot(p, q, preferred_element_type=F32)

    return one(a_high, b_high) + one(a_high, b_low) + one(a_low, b_high)


def mm3_nt(a, b):
    return nt(stack3(a, 1, False), stack3(b, 1, True))


def prepare_k(fields, kfac_ref, coup_ref, k_mat, k_state, k_ends, k_pad):
    n = CK
    flip = jnp.where(iota((n, n), 0) + iota((n, n), 1) == n - 1, 1.0, 0.0).astype(BF)
    flip_cols = jnp.concatenate([flip, flip], 0)
    flip_rows = jnp.concatenate([flip, flip], 1)
    sel_e = entries((8, n), [(0, n - 1, 1.0), (1, n - 2, 1.0)])
    sel_p = entries((8, n), [(2, 0, 1.0), (3, 1, 1.0)])
    pad = jnp.zeros((n - 8, n), F32)
    for f in fields:
        low = kfac_ref[0, f]
        up = jnp.dot(
            jnp.concatenate(split(kfac_ref[1, f]), 1), flip_cols, preferred_element_type=F32
        )
        up = jnp.dot(flip_rows, jnp.concatenate(split(up), 0), preferred_element_type=F32)
        whole = mm3(up, low)
        e_low = entries(
            (8, n),
            [(0, 0, coup_ref[0, 2, f]), (0, 1, coup_ref[2, 2, f]), (1, 0, coup_ref[1, 2, f])],
        )
        e_up = entries(
            (8, n),
            [
                (2, n - 1, coup_ref[0, 3, f]),
                (2, n - 2, coup_ref[2, 3, f]),
                (3, n - 1, coup_ref[1, 3, f]),
            ],
        )
        infl_low = mm3_nt(e_low, low)
        state = -mm3_nt(infl_low + e_up, up)
        k_mat[f] = stack3(whole, 1, True)
        k_state[f] = state
        k_ends[f] = stack3(
            jnp.concatenate([low[n - 1 : n], low[n - 2 : n - 1], whole[0:2], pad[0:4]], 0), 1, False
        )
        k_pad[f] = mm3_nt(sel_p, jnp.concatenate([pad, state], 0)) - mm3_nt(
            sel_e, jnp.concatenate([pad, infl_low], 0)
        )


def chain(count, ends, maps, keep):
    shape = ends(0)[0].shape
    s = [jnp.zeros(shape, F32)] * 2
    tops = []
    for n in range(count):
        e0, e1, p0, p1 = ends(n)
        m = maps(n)
        keep(n, 0, s)
        tops.append(
            [p0 + m[2][0] * s[0] + m[2][1] * s[1], p1 + m[3][0] * s[0] + m[3][1] * s[1]]
        )
        if n < count - 1:
            s = [e0 + m[0][0] * s[0] + m[0][1] * s[1], e1 + m[1][0] * s[0] + m[1][1] * s[1]]
    t = [jnp.zeros(shape, F32)] * 2
    for n in range(count - 1, -1, -1):
        m = maps(n)
        keep(n, 1, t)
        if n > 0:
            q0, q1 = tops[n]
            t = [q0 + m[2][2] * t[0] + m[2][3] * t[1], q1 + m[3][2] * t[0] + m[3][3] * t[1]]


def columns_of(block, first, width):
    def one(a, b):
        return jnp.broadcast_to(
            block[6 * a : 6 * a + 6, first + b : first + b + 1], (FIELDS, width)
        )

    return [
        [one(a, b) if a >= 2 or b < 2 else None for b in range(4)] for a in range(4)
    ]


def main_kernel(
    adj_ref,
    rec_ref,
    res_hbm,
    ifac_ref,
    kfac_hbm,
    coup_ref,
    count_ref,
    cell_ref,
    weight_ref,
    z_hbm,
    k_st,
    k_state,
    table,
    where_ref,
    place,
    outgoing,
    incoming,
    info_out,
    info_in,
    rest,
    acc,
    acc_rest,
    rs_in,
    ag_in,
    x,
    i_mat,
    i_state,
    i_ends,
    i_maps,
    i_out,
    i_in,
    s_out,
    s_in,
    k_mat,
    k_ends,
    k_pad,
    k_all,
    xk,
    info_send,
    info_recv,
    a2a_send,
    a2a_recv,
    rs_send,
    rs_recv,
    ag_send,
    ag_recv,
    map_send,
    map_recv,
    end_send,
    end_recv,
    st_send,
    st_recv,
    k_send,
    k_recv,
    res_ref,
    kfac_ref,
    load_sem,
):
    load_res = pltpu.make_async_copy(res_hbm, res_ref, load_sem.at[0])
    load_kfac = pltpu.make_async_copy(kfac_hbm, kfac_ref, load_sem.at[1])
    load_res.start()
    load_kfac.start()
    line, block = lax.axis_index("line"), lax.axis_index("block")
    barrier = pltpu.get_barrier_semaphore()
    for d in range(1, LINES):
        pl.semaphore_signal(
            barrier, inc=1, device_id={"line": lax.rem(line + d, LINES)}, device_id_type=MESH
        )
    for d in range(1, BLOCKS):
        pl.semaphore_signal(
            barrier, inc=1, device_id={"block": lax.rem(block + d, BLOCKS)}, device_id_type=MESH
        )

    def to_line(d, src, dst, send, recv):
        return pltpu.make_async_remote_copy(
            src_ref=src,
            dst_ref=dst,
            send_sem=send.at[d],
            recv_sem=recv.at[d],
            device_id={"line": lax.rem(line + d, LINES)},
            device_id_type=MESH,
        )

    def to_block(d, src, dst, send, recv):
        return pltpu.make_async_remote_copy(
            src_ref=src,
            dst_ref=dst,
            send_sem=send.at[d],
            recv_sem=recv.at[d],
            device_id={"block": lax.rem(block + d, BLOCKS)},
            device_id_type=MESH,
        )

    def peer(d):
        return lax.rem(block + d, BLOCKS)

    def info_copy(d):
        return to_block(d, info_out.at[peer(d)], info_in.at[block], info_send, info_recv)

    def slot_copy(d):
        return to_block(d, outgoing.at[peer(d)], incoming.at[block], a2a_send, a2a_recv)

    def rs_copy(d):
        return to_block(d, acc_rest.at[peer(d)], rs_in.at[block], rs_send, rs_recv)

    def ag_copy(d):
        return to_block(d, ag_in.at[block], ag_in.at[block], ag_send, ag_recv)

    def over_peers(action):
        def step(d, carry):
            action(d)
            return carry

        lax.fori_loop(1, BLOCKS, step, 0)

    hot = jnp.int32(0)
    for o in range(BLOCKS):
        hot = jnp.where(count_ref[o] == CAP, o, hot)

    for p in range(BLOCKS):
        info_out[p, 0:1, :] = cell_ref[p : p + 1, HEAD:].astype(F32)
        for a in range(3):
            info_out[p, a + 1 : a + 2, :] = weight_ref[a, p : p + 1, HEAD:]
    gather_table(adj_ref, table)
    i, j, k = cell_parts(rec_ref[...])
    where_ref[0] = (j & 7) * CI + i
    where_ref[1] = (j >> 3) * CK + k
    for a, part in enumerate(donor_parts(cell_ref[...])):
        place[a] = part
    prepare_i(ifac_ref, coup_ref, i_mat, i_state, i_ends, i_maps.at[line])
    outgoing[:, FIELDS * PIECES :, :] = jnp.zeros((BLOCKS, 32 - FIELDS * PIECES, 256), F32)

    def owner_step(t, carry):
        owners = [peer(2 * t), peer(2 * t + 1)]
        group_row, slot_row = [
            jnp.concatenate([where_ref[a, pl.ds(o, 1), 0:HEAD] for o in owners], 1)
            for a in range(2)
        ]
        rows = gather_slots(adj_ref, table, group_row, slot_row)
        for n, o in enumerate(owners):
            live = iota((1, HEAD), 1) < count_ref[o]
            for f in range(FIELDS):
                row = jnp.where(live, rows[f][:, n * HEAD : (n + 1) * HEAD], 0.0)
                for q in range(PIECES):
                    at = q * FIELDS + f
                    outgoing[o, at : at + 1, :] = row[:, q * 256 : (q + 1) * 256]
        return carry

    lax.fori_loop(0, EARLY, owner_step, 0)
    incoming[block] = outgoing[block]
    for f, row in enumerate(
        gather_slots(adj_ref, table, where_ref[0, pl.ds(hot, 1), HEAD:], where_ref[1, pl.ds(hot, 1), HEAD:])
    ):
        rest[f : f + 1, :] = row

    pl.semaphore_wait(barrier, LINES + BLOCKS - 2)
    over_peers(lambda d: info_copy(d).start())

    def early_step(d, carry):
        slot_copy(d).start()
        return carry

    lax.fori_loop(1, 2 * EARLY, early_step, 0)
    map_copies = [
        to_line(d, i_maps.at[line], i_maps.at[line], map_send, map_recv) for d in range(1, LINES)
    ]
    for copy in map_copies:
        copy.start()
    info_in[block] = info_out[block]

    def late_step(d, carry):
        owner_step(d, carry)
        slot_copy(2 * d).start()
        slot_copy(2 * d + 1).start()
        return carry

    lax.fori_loop(EARLY, BLOCKS // 2, late_step, 0)

    acc[...] = jnp.zeros_like(acc)

    def source_step(t, carry):
        sources = [lax.rem(block + BLOCKS - TOGETHER * t - n, BLOCKS) for n in range(TOGETHER)]

        @pl.when(t > 0)
        def _():
            slot_copy(TOGETHER * t).wait_recv()

        for n in range(1, TOGETHER):
            slot_copy(TOGETHER * t + n).wait_recv()

        @pl.when(t == REST_AT)
        def _():
            over_peers(lambda d: info_copy(d).wait())
            info = info_in[hot]
            found = scatter_slots(
                [rest[f : f + 1, :] for f in range(FIELDS)],
                *donor_parts(info[0:1].astype(jnp.int32)),
                info[1:2],
                info[2:3],
                info[3:4],
            )
            for p in range(BLOCKS):
                acc_rest[p] = found[p * PART : (p + 1) * PART]
            rs_in[block] = acc_rest[block]
            over_peers(lambda d: rs_copy(d).start())

        @pl.when(t == GRID_AT)
        def _():
            over_peers(lambda e: rs_copy(e).wait())
            total = rs_in[0]
            for p in range(1, BLOCKS):
                total = total + rs_in[p]
            ag_in[block] = total
            over_peers(lambda e: ag_copy(e).start())

        def row(ref, a):
            return jnp.concatenate([ref[a, pl.ds(s, 1), 0:HEAD] for s in sources], 1)

        values = [incoming[s] for s in sources]
        acc[...] += scatter_slots(
            [
                jnp.concatenate(
                    [v[q * FIELDS + f : q * FIELDS + f + 1] for v in values for q in range(PIECES)],
                    1,
                )
                for f in range(FIELDS)
            ],
            *[row(place, a) for a in range(3)],
            *[row(weight_ref, a) for a in range(3)],
        )
        return carry

    lax.fori_loop(0, BLOCKS // TOGETHER, source_step, 0)
    over_peers(lambda d: slot_copy(d).wait_send())
    over_peers(lambda d: ag_copy(d).wait())

    load_res.wait()
    load_kfac.wait()
    n = FIELDS * CI
    for j in range(CJ):
        total = res_ref[:, j].reshape(n, CK)
        for r, c in ((j, 0), (j - 7, CK)):
            if 0 <= r < 8:
                more = jnp.concatenate([ag_in[2 * r, :, c : c + CK], ag_in[2 * r + 1, :, c : c + CK]], 0)
                more = jnp.where(hot == block, more, 0.0)
                total = total + acc[r * n : (r + 1) * n, c : c + CK] + more
        x[:, j * CK : (j + 1) * CK] = total
    x[:, CJ * CK :] = jnp.zeros((n, CK), F32)

    ends = mm_fast(i_ends[...], x[...])
    for c in range(LINES):
        i_out[c] = ends[:, c * 256 : (c + 1) * 256]
    i_in[line] = i_out[line]
    end_copies = [
        to_line(d, i_out.at[(line + d) % LINES], i_in.at[line], end_send, end_recv)
        for d in (4, 5, 3, 6, 2, 7, 1)
    ]
    for copy in end_copies:
        copy.start()
    x[...] = mm_fast(i_mat[...], x[...])
    k_refs = (kfac_ref, coup_ref, k_mat, k_state, k_ends, k_pad)
    prepare_k(range(0, 3), *k_refs)
    for copy in map_copies:
        copy.wait()
    for copy in end_copies:
        copy.wait()

    def i_end(s):
        return [i_in[s, 6 * a : 6 * a + 6, :] for a in range(4)]

    i_cols = [columns_of(i_maps[s], 0, 256) for s in range(LINES)]

    def i_keep(s, up, state):
        for a in range(2):
            at = 12 * up + 6 * a
            s_out[s, at : at + 6, :] = state[a]

    chain(LINES, i_end, lambda s: i_cols[s], i_keep)
    s_in[line] = s_out[line]
    st_copies = [
        to_line(d, s_out.at[(line + d) % LINES], s_in.at[line], st_send, st_recv)
        for d in (4, 5, 3, 6, 2, 7, 1)
    ]
    for copy in st_copies:
        copy.start()
    prepare_k(range(3, 6), *k_refs)
    for copy in st_copies:
        copy.wait()
    for c in range(LINES):
        part = x[:, c * 256 : (c + 1) * 256] + mm_fast(i_state[...], s_in[c])
        for jj in range(2):
            j = 2 * c + jj
            for f in range(FIELDS):
                xk[f, j * 8 : j * 8 + 8, :] = part[f * 8 : f * 8 + 8, jj * CK : (jj + 1) * CK]

    for f in range(FIELDS):
        found = nt(k_ends[f], stack3(xk[f], 1, True)) + k_pad[f]
        for a in range(4):
            k_all[block, 6 * a + f : 6 * a + f + 1, :] = found[a : a + 1]
    k_copies = [
        pltpu.make_async_remote_copy(
            src_ref=k_all.at[block],
            dst_ref=k_all.at[block],
            send_sem=k_send.at[d],
            recv_sem=k_recv.at[d],
            device_id={"block": (block + d) % BLOCKS},
            device_id_type=MESH,
        )
        for d in (10, 9, 11, 6, 14, 5, 7, 13, 2, 8, 15, 3, 1, 4, 12)
    ]
    for copy in k_copies:
        copy.start()
    for f in range(FIELDS):
        xk[f] = nt(stack3(xk[f], 1, False), k_mat[f])
    store_z = pltpu.make_async_copy(xk, z_hbm, load_sem.at[2])
    store_z.start()
    for copy in k_copies:
        copy.wait()

    def k_end(s):
        return [k_all[s, 6 * a : 6 * a + 6, :] for a in range(4)]

    k_cols = [columns_of(k_all[s], 120, CK) for s in range(BLOCKS)]
    kept = [[jnp.zeros((FIELDS, CK), F32)] * 2 for _ in range(2)]

    def k_keep(s, up, state):
        kept[up] = [jnp.where(block == s, state[a], kept[up][a]) for a in range(2)]

    chain(BLOCKS, k_end, lambda s: k_cols[s], k_keep)
    k_st[...] = jnp.zeros_like(k_st)
    for f in range(FIELDS):
        for a in range(4):
            k_st[f, a : a + 1, :] = kept[a // 2][a % 2][f : f + 1]
    store_z.wait()


def finish_kernel(z_ref, st_ref, state_ref, out_ref):
    for f in range(FIELDS):
        done = z_ref[f] + mm_tn(st_ref[f], state_ref[f])
        out_ref[f] = done[0 : CJ * CI].reshape(CJ, CI, CK)


def finish(z, states, state_map):
    vmem = pl.BlockSpec(memory_space=pltpu.VMEM)
    return pl.pallas_call(
        finish_kernel,
        out_shape=jax.ShapeDtypeStruct((FIELDS, CJ, CI, CK), F32),
        in_specs=[vmem] * 3,
        out_specs=vmem,
        name="finish",
    )(z, states, state_map)


def sweep(
    adjoint,
    receptor_cell,
    residual,
    i_factors,
    k_factors,
    couplings,
    send_count,
    donor_cell,
    donor_weight,
):
    vmem, smem = pl.BlockSpec(memory_space=pltpu.VMEM), pl.BlockSpec(memory_space=pltpu.SMEM)
    hbm = pl.BlockSpec(memory_space=pl.ANY)
    n = FIELDS * CI
    dma = pltpu.SemaphoreType.DMA
    return pl.pallas_call(
        main_kernel,
        out_shape=[
            jax.ShapeDtypeStruct((FIELDS, CK, CK), F32),
            jax.ShapeDtypeStruct((FIELDS, 8, CK), F32),
            jax.ShapeDtypeStruct((FIELDS, 8, CK), F32),
        ],
        in_specs=[vmem] * 2 + [hbm, vmem, hbm, smem, smem] + [vmem] * 2,
        out_specs=[hbm, vmem, vmem],
        scratch_shapes=[
            pltpu.VMEM((TABLED * 64, 512), BF),
            pltpu.VMEM((2, BLOCKS, CAP), jnp.int32),
            pltpu.VMEM((3, BLOCKS, CAP), jnp.int32),
            pltpu.VMEM((BLOCKS, 32, 256), F32),
            pltpu.VMEM((BLOCKS, 32, 256), F32),
            pltpu.VMEM((BLOCKS, 4, REST), F32),
            pltpu.VMEM((BLOCKS, 4, REST), F32),
            pltpu.VMEM((FIELDS, REST), F32),
            pltpu.VMEM((384, 256), F32),
            pltpu.VMEM((BLOCKS, PART, 256), F32),
            pltpu.VMEM((BLOCKS, PART, 256), F32),
            pltpu.VMEM((BLOCKS, PART, 256), F32),
            pltpu.VMEM((n, 16 * CK), F32),
            pltpu.VMEM((n, n), F32),
            pltpu.VMEM((n, 24), F32),
            pltpu.VMEM((24, n), F32),
            pltpu.VMEM((LINES, 24, CK), F32),
            pltpu.VMEM((LINES, 24, 256), F32),
            pltpu.VMEM((LINES, 24, 256), F32),
            pltpu.VMEM((LINES, 24, 256), F32),
            pltpu.VMEM((LINES, 24, 256), F32),
            pltpu.VMEM((FIELDS, CK, 3 * CK), BF),
            pltpu.VMEM((FIELDS, 8, 3 * CK), BF),
            pltpu.VMEM((FIELDS, 8, CK), F32),
            pltpu.VMEM((BLOCKS, 24, CK), F32),
            pltpu.VMEM((FIELDS, CK, CK), F32),
        ]
        + [dma((BLOCKS,))] * 8
        + [dma((LINES,))] * 6
        + [dma((BLOCKS,))] * 2
        + [
            pltpu.VMEM((FIELDS, CJ, CI, CK), F32),
            pltpu.VMEM((2, FIELDS, CK, CK), F32),
            dma((3,)),
        ],
        compiler_params=pltpu.CompilerParams(
            vmem_limit_bytes=56 * 2**20, collective_id=0, has_side_effects=True
        ),
        name="sweep",
    )(
        adjoint,
        receptor_cell,
        residual,
        i_factors,
        k_factors,
        couplings,
        send_count,
        donor_cell,
        donor_weight,
    )


def per_device(
    residual,
    adjoint,
    i_factors,
    k_factors,
    couplings,
    receptor_cell,
    send_count,
    donor_cell,
    donor_weight,
):
    update = finish(*sweep(
        adjoint.transpose(0, 2, 1, 3),
        receptor_cell[0, 0],
        residual.transpose(0, 2, 1, 3),
        i_factors[0],
        k_factors[0],
        couplings[0, 0].transpose(1, 0, 2),
        send_count[0, 0],
        donor_cell[0, 0],
        donor_weight[0, 0],
    ))
    return update.transpose(0, 2, 1, 3)


def solution(mesh):
    return jax.shard_map(
        per_device,
        mesh=mesh,
        in_specs=(
            P(None, "line", None, "block"),
            P(None, "line", None, "block"),
            P("block", None, None, "line", None),
            P("line", None, None, "block", None),
            P("line", "block", None, None, None),
            P("line", "block", None, None),
            P("line", "block", None),
            P("line", "block", None, None),
            P("line", "block", None, None, None),
        ),
        out_specs=P(None, "line", None, "block"),
        check_vma=False,
    )
```
